256 devices in a mesh: dp: 4 (over x_hi, core), ctx: 64 (over x_lo, y, z).
Axes of the slice: x: 4 (x_hi: 2, x_lo: 2; x = x_hi * 2 + x_lo), y: 4, z: 8, core: 2. Of those that a mesh axis runs over, the one named last changes fastest.
Arguments:
- hidden: bfloat16 [49152, 1024], P(('dp', 'ctx')), parts along dimension 0, may hold values from -6 to 6
- flow_input: bfloat16 [64, 49152], P(None, ('dp', 'ctx')), parts along dimension 1, may hold values from -6 to 6
- w_query: bfloat16 [1024, 512], replicated, may hold values from -6 to 6
- w_key: bfloat16 [1024, 512], replicated, may hold values from -6 to 6
- w_value: bfloat16 [1024, 512], replicated, may hold values from -0.1875 to 0.1875
- w_output: bfloat16 [512, 1024], replicated, may hold values from -0.25 to 0.25
- w_up: bfloat16 [1024, 2048], replicated, may hold values from -0.1875 to 0.1875
- w_down: bfloat16 [2048, 1024], replicated, may hold values from -0.125 to 0.125
- w_shift: bfloat16 [64, 1024], replicated, may hold values from -0.1875 to 0.1875
- w_scale: bfloat16 [64, 1024], replicated, may hold values from -0.09375 to 0.09375
Outputs:
- latent: float32 [64, 49152], P(None, ('dp', 'ctx')), parts along dimension 1
- log_det: float32 [49152], P(('dp', 'ctx')), parts along dimension 0
The draws below stay inside these ranges and needn't reach their ends.
There are 4 independent parts, one for each index of `dp`. The reference program is written for one: setup_inputs(seed, part) draws one part's arguments, and reference() takes and returns one part's arrays. A program takes and returns all parts, laid end to end along the dimension named above; an argument that names none is the same for every part. Nothing has to cross between parts.
All inputs are finite; a program needn't handle non-finite values.
Results may differ from the reference program's by a relative error of at most 0.015.
Values may be sent and summed in bfloat16 or wider, within the bound.
No kernel may reach another device: no remote copies, remote signals or barrier semaphores. Data moves between devices by JAX's collectives and lax.ppermute only.
A program may use at most 128 MiB of HBM per device.

```python
import math
import jax
import jax.numpy as jnp
from jax import lax

D = 1024
HEADS = 4
HEAD = 128
FF = 2048
C = 64
TOKENS = 12288


def shared_base(key):
    return jax.random.truncated_normal(key, -4.0, 4.0, (D, HEADS * HEAD), jnp.float32)


def draw_w_key(key, part):
    base = shared_base(key)
    key = jax.random.fold_in(key, 3)
    extra = jax.random.truncated_normal(key, -4.0, 4.0, (D, HEADS * HEAD), jnp.float32)
    values = (0.9 * base + 0.45 * extra) * 1.4 * D ** (-0.5)
    return jnp.clip(values, -6.0, 6.0).astype(jnp.bfloat16)


def draw_w_query(key, part):
    key = jax.random.fold_in(key, 5)
    own = jax.random.truncated_normal(key, -4.0, 4.0, (D, HEADS * HEAD), jnp.float32)
    values = own * 2.0 * D ** (-0.5)
    return jnp.clip(values, -6.0, 6.0).astype(jnp.bfloat16)


def shard_levels(own_key, extent, cuts, smallest, top_value):
    level = 1.0
    for dim, shards_of in cuts:
        heights = jax.random.uniform(jax.random.fold_in(jax.random.fold_in(own_key, 6), dim), (shards_of,), jnp.float32, smallest / len(cuts), top_value / len(cuts))
        level = level * jnp.repeat(jnp.exp(heights), extent[dim] // shards_of).reshape((-1,) + (1,) * (len(extent) - 1 - dim))
    return level


def normal_values(rng, shape, deviation, most, split=(), held_as=jnp.bfloat16):
    level = shard_levels(rng, shape, split, -0.22, 0.18) if split else 1.0
    values = jax.random.normal(rng, shape, jnp.float32) * deviation * level
    return jnp.minimum(jnp.maximum(values, -most), most).astype(held_as)


def setup_inputs(seed: int = 0, part: int = 0) -> dict:
    seeds = jax.random.split(jax.random.key(seed), 11)
    part_splits = jax.random.split(jax.random.fold_in(seeds[10], part), 11)
    hidden = normal_values(part_splits[0], (TOKENS, D), 1.0, 6.0, ((0, 64),))
    flow_input = normal_values(part_splits[1], (C, TOKENS), 1.0, 6.0, ((1, 64),))
    w_query = draw_w_query(jax.random.fold_in(seeds[10], 71), part)
    w_key = draw_w_key(jax.random.fold_in(seeds[10], 71), part)
    w_value = normal_values(seeds[4], (D, HEADS * HEAD), D ** -0.5, 0.1875)
    w_output = normal_values(seeds[5], (HEADS * HEAD, D), (HEADS * HEAD) ** -0.5, 0.25)
    w_up = normal_values(seeds[6], (D, FF), D ** -0.5, 0.1875)
    w_down = normal_values(seeds[7], (FF, D), FF ** -0.5, 0.125)
    w_shift = normal_values(seeds[8], (C, D), D ** -0.5, 0.1875)
    w_scale = normal_values(seeds[9], (C, D), (4 * D) ** -0.5, 0.09375)
    return {"hidden": hidden, "flow_input": flow_input, "w_query": w_query, "w_key": w_key, "w_value": w_value, "w_output": w_output, "w_up": w_up, "w_down": w_down, "w_shift": w_shift, "w_scale": w_scale}


epsilon = 1e-05
masked_score = -1e+30

def layer_norm(values):
    mean = lax.optimization_barrier(jnp.mean(values, axis=-1, keepdims=True))
    centred = values - mean
    spread = lax.optimization_barrier(jnp.mean(centred * centred, axis=-1, keepdims=True))
    return centred * lax.rsqrt(spread + epsilon)

def reference(hidden, flow_input, w_query, w_key, w_value, w_output, w_up, w_down, w_shift, w_scale):
    length = hidden.shape[0]
    residual = hidden.astype(jnp.float32)
    normed = layer_norm(residual).astype(jnp.bfloat16)
    queries = jnp.dot(normed, w_query, preferred_element_type=jnp.float32).astype(jnp.bfloat16)
    keys = jnp.dot(normed, w_key, preferred_element_type=jnp.float32).astype(jnp.bfloat16)
    values = jnp.dot(normed, w_value, preferred_element_type=jnp.float32).astype(jnp.bfloat16)
    key_heads = keys.reshape(length, HEADS, HEAD).astype(jnp.float32)
    value_heads = values.reshape(length, HEADS, HEAD).astype(jnp.float32)
    places = jnp.arange(length, dtype=jnp.int32)
    block = math.gcd(length, 512)
    scale = HEAD ** (-0.5)

    def one_block(block_index):
        first_row = (block_index * block).astype(jnp.int32)
        query_block = lax.dynamic_slice_in_dim(queries, first_row, block, 0)
        query_block = query_block.reshape(block, HEADS, HEAD).astype(jnp.float32)
        query_place = first_row + jnp.arange(block, dtype=jnp.int32)
        scores = jnp.einsum('qhd,khd->hqk', query_block, key_heads) * scale
        allowed = places[None, None, :] <= query_place[None, :, None]
        scores = jnp.where(allowed, scores, masked_score)
        top = lax.optimization_barrier(jnp.max(scores, axis=-1, keepdims=True))
        weights = jnp.where(allowed, jnp.exp(scores - top), 0.0)
        total = lax.optimization_barrier(jnp.sum(weights, axis=-1))
        rounded = lax.optimization_barrier(weights.astype(jnp.bfloat16)).astype(jnp.float32)
        mixed = jnp.einsum('hqk,khd->qhd', rounded, value_heads) / jnp.transpose(total)[:, :, None]
        return mixed.reshape(block, HEADS * HEAD)
    attended = lax.map(one_block, jnp.arange(length // block, dtype=jnp.int32))
    attended = attended.reshape(length, HEADS * HEAD).astype(jnp.bfloat16)
    first = residual + jnp.dot(attended, w_output, preferred_element_type=jnp.float32)
    inner = layer_norm(first).astype(jnp.bfloat16)
    expanded = jax.nn.gelu(jnp.dot(inner, w_up, preferred_element_type=jnp.float32)).astype(jnp.bfloat16)
    second = first + jnp.dot(expanded, w_down, preferred_element_type=jnp.float32)
    features = layer_norm(second).astype(jnp.bfloat16)
    shift = lax.dot_general(w_shift, features, (((1,), (1,)), ((), ())), preferred_element_type=jnp.float32)
    log_scale = lax.dot_general(w_scale, features, (((1,), (1,)), ((), ())), preferred_element_type=jnp.float32)
    moved = (flow_input.astype(jnp.float32) - shift) * jnp.exp(-log_scale)
    token_det = -lax.optimization_barrier(jnp.sum(log_scale, axis=0))
    return (moved[:, ::-1], token_det[::-1])
```

```python
import functools

import jax
import jax.numpy as jnp
from jax import lax
from jax.experimental import pallas as pl
from jax.experimental.pallas import tpu as pltpu
from jax.sharding import Mesh, PartitionSpec as P

HEADS = 4
HEAD = 128
epsilon = 1e-05
masked_score = -2e30
lowest = -1e30
POWER = HEAD**-0.5 * 1.4426950408889634
bf16 = jnp.bfloat16
f32 = jnp.float32
VMEM_LIMIT = 50 * 1024 * 1024

XL, Y, Z = 2, 4, 8
PLANES = XL * Y
TOKENS = 192
PIECE = TOKENS // 2
ROWS = PLANES * PIECE
TILE = 2 * TOKENS


def layer_norm(values):
    mean = jnp.mean(values, axis=-1, keepdims=True)
    centred = values - mean
    spread = jnp.mean(centred * centred, axis=-1, keepdims=True)
    return centred * lax.rsqrt(spread + epsilon)


def vmem():
    return pl.BlockSpec(memory_space=pltpu.VMEM)


def smem():
    return pl.BlockSpec(memory_space=pltpu.SMEM)


def params():
    return pltpu.CompilerParams(vmem_limit_bytes=VMEM_LIMIT)


def key_value_kernel(place, own, other, w_key, w_value, slots, normed):
    core = place[0]
    for part, rows in enumerate((own, other)):
        normed[part * PIECE : (part + 1) * PIECE, :] = layer_norm(rows[...].astype(f32)).astype(bf16)
    for column, weight in enumerate((w_key, w_value)):
        made = jnp.dot(normed[...], weight[...], preferred_element_type=f32).astype(bf16)
        for part in range(2):
            sequence = core if part == 0 else 1 - core
            for head in range(HEADS):
                slots[sequence * HEADS + head, :, column * HEAD : (column + 1) * HEAD] = made[
                    part * PIECE : (part + 1) * PIECE, head * HEAD : (head + 1) * HEAD
                ]


def query_kernel(place, normed, w_query, slots):
    core = place[0]
    made = jnp.dot(normed[...], w_query[...], preferred_element_type=f32).astype(bf16)
    for part in range(2):
        sequence = core if part == 0 else 1 - core
        for head in range(HEADS):
            slots[sequence * HEADS + head] = made[
                part * PIECE : (part + 1) * PIECE, head * HEAD : (head + 1) * HEAD
            ]


def attend_kernel(parts, sources, first, last, *refs):
    refs = list(refs)
    place = refs.pop(0)
    queries = refs.pop(0)
    segments = [refs.pop(0) for _ in parts]
    if first:
        top_in = total_in = numer_in = None
    else:
        top_in, total_in, numer_in = refs[:3]
        refs = refs[3:]
    core = place[0]
    ones = jnp.ones((2 * TOKENS, HEAD), bf16)
    row = lax.broadcasted_iota(jnp.int32, (TILE, 1), 0)
    row_side = (row % TOKENS) // PIECE
    row_half = jnp.where(row_side == 0, core, 1 - core)
    row_place = (row // TOKENS) * (Z * TOKENS) + row_half * PIECE + row % PIECE
    key = lax.broadcasted_iota(jnp.int32, (1, 2 * TOKENS), 1)
    key_place = (key // PIECE) * (Z * TOKENS) + key % PIECE + core * PIECE
    for tile in range(4):
        rows = slice(tile * TILE, (tile + 1) * TILE)
        tile_queries = queries[rows, :]
        scores = []
        for segment, part, source in zip(segments, parts, sources):
            groups = min(2, tile + 1 - 2 * part)
            if groups <= 0:
                continue
            count = groups * TOKENS
            product = lax.dot_general(
                tile_queries,
                segment[:count, :HEAD],
                (((1,), (1,)), ((), ())),
                preferred_element_type=f32,
            )
            if 2 * part + groups - 1 == tile:
                shift = place[1 + source] * TOKENS
                offset = (2 * (tile - 2 * part)) * (Z * TOKENS)
                allowed = key_place[:, :count] + shift <= row_place + offset
                product = jnp.where(allowed, product, masked_score)
            scores.append((segment, count, product))
        top = lowest if first else top_in[rows, :1]
        new_top = functools.reduce(
            jnp.maximum, [jnp.max(product, axis=-1, keepdims=True) for _, _, product in scores], top
        )
        sums = None
        for segment, count, product in scores:
            weights = jnp.exp2((product - new_top) * POWER).astype(bf16)
            with_ones = jnp.concatenate([segment[:count, HEAD:], ones[:count]], axis=1)
            term = jnp.dot(weights, with_ones, preferred_element_type=f32)
            sums = term if sums is None else sums + term
        numer, total = sums[:, :HEAD], sums[:, HEAD:]
        if not first:
            factor = jnp.exp2((top - new_top) * POWER)
            numer = numer + numer_in[rows, :] * factor
            total = total + total_in[rows, :] * factor
        new_top = jnp.broadcast_to(new_top, (TILE, HEAD))
        if not last:
            top_out, total_out, numer_out = refs
            top_out[rows, :] = new_top
            total_out[rows, :] = total
            numer_out[rows, :] = numer
        else:
            some = total > 0
            mixed = numer / jnp.where(some, total, 1.0)
            level = jnp.where(some, new_top * POWER + jnp.log2(jnp.where(some, total, 1.0)), lowest)
            high = level.astype(bf16)
            rest = level - high.astype(f32)
            middle = rest.astype(bf16)
            low = (rest - middle.astype(f32)).astype(bf16)
            lane = lax.broadcasted_iota(jnp.int32, (TILE, HEAD), 1)
            level = jnp.where(lane == 0, high, jnp.where(lane == 1, middle, low))
            for plane in range(2):
                for side in range(2):
                    start = plane * TOKENS + side * PIECE
                    out = refs[side]
                    out[2 * tile + plane, :, :HEAD] = mixed[start : start + PIECE].astype(bf16)
                    out[2 * tile + plane, :, HEAD:] = level[start : start + PIECE]


def attend(place, queries, segments, parts, sources, state, last):
    first = state is None
    keys = sum(segment.shape[0] for segment in segments)
    stat = jax.ShapeDtypeStruct((2 * ROWS, HEAD), f32)
    done = jax.ShapeDtypeStruct((PLANES, PIECE, 2 * HEAD), bf16)
    operands = [place, queries, *segments, *(state or ())]
    return pl.pallas_call(
        functools.partial(attend_kernel, parts, sources, first, last),
        out_shape=[done] * 2 if last else [stat] * 3,
        in_specs=[smem()] + [vmem()] * (len(operands) - 1),
        out_specs=[vmem()] * (2 if last else 3),
        compiler_params=params(),
        cost_estimate=pl.CostEstimate(
            flops=2 * ROWS * keys * HEAD * 6,
            bytes_accessed=4_000_000,
            transcendentals=ROWS * keys,
        ),
    )(*operands)


def shift_by(count, step):
    return [(index, (index + step) % count) for index in range(count)]


def merge(mine, theirs):
    def level(block):
        return sum(block[..., HEAD + index : HEAD + index + 1].astype(f32) for index in range(3))

    first, second = level(mine), level(theirs)
    top = jnp.maximum(first, second)
    first, second = jnp.exp2(first - top), jnp.exp2(second - top)
    both = first * mine[..., :HEAD].astype(f32) + second * theirs[..., :HEAD].astype(f32)
    return (both / (first + second)).astype(bf16)


def on_device(
    hidden, flow_input, w_query, w_key, w_value, w_output, w_up, w_down, w_shift, w_scale
):
    core = lax.axis_index("core")
    other_core = shift_by(2, 1)
    own = lax.dynamic_slice_in_dim(hidden, core * PIECE, PIECE, 0)
    other = lax.ppermute(
        lax.dynamic_slice_in_dim(hidden, (1 - core) * PIECE, PIECE, 0), "core", other_core
    )
    own_flow = lax.dynamic_slice_in_dim(flow_input, core * PIECE, PIECE, 1)
    other_flow = lax.ppermute(
        lax.dynamic_slice_in_dim(flow_input, (1 - core) * PIECE, PIECE, 1), "core", other_core
    )
    z = lax.axis_index("z")
    up_steps = [(z - step) % Z - z for step in range(5)]
    down_steps = [(z + step) % Z - z for step in range(4)]
    place = jnp.stack([core, *up_steps, *down_steps]).astype(jnp.int32)

    slots, normed = pl.pallas_call(
        key_value_kernel,
        out_shape=[
            jax.ShapeDtypeStruct((PLANES, PIECE, 2 * HEAD), bf16),
            jax.ShapeDtypeStruct((TOKENS, hidden.shape[1]), bf16),
        ],
        in_specs=[smem()] + [vmem()] * 4,
        out_specs=[vmem()] * 2,
        compiler_params=params(),
    )(place, own, other, w_key, w_value)
    keys_values = lax.all_to_all(slots, ("xl", "y"), 0, 0, tiled=True).reshape(ROWS, 2 * HEAD)
    slots = pl.pallas_call(
        query_kernel,
        out_shape=jax.ShapeDtypeStruct((PLANES, PIECE, HEAD), bf16),
        in_specs=[smem()] + [vmem()] * 2,
        out_specs=vmem(),
        compiler_params=params(),
    )(place, normed, w_query)
    own_queries = lax.all_to_all(slots, ("xl", "y"), 0, 0, tiled=True)
    other_queries = lax.ppermute(own_queries, "core", other_core)
    queries = jnp.stack([own_queries, other_queries], axis=1).reshape(2 * ROWS, HEAD)

    half = ROWS // 2
    up = [keys_values[:half], keys_values[half:]]
    down = list(up)
    state = attend(place, queries, up, (0, 1), (0, 0), None, False)
    for step in range(1, 4):
        for part in range(2):
            up[part] = lax.ppermute(up[part], "z", shift_by(Z, 1))
            down[part] = lax.ppermute(down[part], "z", shift_by(Z, -1))
        state = attend(
            place,
            queries,
            up + down,
            (0, 1, 0, 1),
            (step, step, 5 + step, 5 + step),
            state,
            False,
        )
    far = [
        lax.ppermute(up[0], "z", shift_by(Z, 1)),
        lax.ppermute(down[1], "z", shift_by(Z, -1)),
    ]
    mine, others = attend(place, queries, far, (0, 1), (4, 4), state, True)
    attended = merge(mine, lax.ppermute(others, "core", other_core))
    attended = lax.all_to_all(attended, ("xl", "y"), 0, 0, tiled=True)
    attended = attended.reshape(2, HEADS, PIECE, HEAD)
    attended = jnp.where(core == 0, attended, attended[::-1])
    attended = jnp.transpose(attended, (0, 2, 1, 3)).reshape(TOKENS, HEADS * HEAD)

    residual = jnp.concatenate([own, other], axis=0).astype(f32)
    first = residual + jnp.dot(attended, w_output, preferred_element_type=f32)
    inner = layer_norm(first).astype(bf16)
    expanded = jax.nn.gelu(jnp.dot(inner, w_up, preferred_element_type=f32)).astype(bf16)
    second = first + jnp.dot(expanded, w_down, preferred_element_type=f32)
    features = layer_norm(second).astype(bf16)
    shift = lax.dot_general(
        w_shift, features, (((1,), (1,)), ((), ())), preferred_element_type=f32
    )
    log_scale = lax.dot_general(
        w_scale, features, (((1,), (1,)), ((), ())), preferred_element_type=f32
    )
    flow = jnp.concatenate([own_flow, other_flow], axis=1).astype(f32)
    moved = (flow - shift) * jnp.exp(-log_scale)
    token_det = -jnp.sum(log_scale, axis=0, keepdims=True)
    det_high = token_det.astype(bf16)
    det_low = (token_det - det_high.astype(f32)).astype(bf16)
    sent = jnp.concatenate([moved.astype(bf16), det_high, det_low], axis=0)
    blocks = XL * Y * Z
    same = [
        (side * blocks + index, side * blocks + blocks - 1 - index)
        for side in range(2)
        for index in range(blocks)
    ]
    crossed = [
        (side * blocks + index, (1 - side) * blocks + blocks - 1 - index)
        for side in range(2)
        for index in range(blocks)
    ]
    axes = ("core", "xl", "y", "z")
    from_same = lax.ppermute(sent[:, :PIECE], axes, same)
    from_crossed = lax.ppermute(sent[:, PIECE:], axes, crossed)
    arrived = jnp.where(
        core == 0,
        jnp.concatenate([from_crossed, from_same], axis=1),
        jnp.concatenate([from_same, from_crossed], axis=1),
    )
    arrived = arrived.astype(f32).reshape(-1, 2, PIECE)[:, :, ::-1].reshape(-1, TOKENS)
    return (arrived[:64], arrived[64] + arrived[65])


def solution(mesh):
    parts = Mesh(mesh.devices.reshape(2, 2, XL, Y, Z), ("xh", "core", "xl", "y", "z"))
    everywhere = ("xh", "core", "xl", "y", "z")
    in_specs = (P(everywhere, None), P(None, everywhere)) + (P(),) * 8
    out_specs = (P(None, everywhere), P(everywhere))
    return jax.shard_map(
        on_device, mesh=parts, in_specs=in_specs, out_specs=out_specs, check_vma=False
    )
```

```python
import functools

import jax
import jax.numpy as jnp
from jax import lax
from jax.experimental import pallas as pl
from jax.experimental.pallas import tpu as pltpu
from jax.sharding import Mesh, PartitionSpec as P

HEADS = 4
HEAD = 128
WIDTH = 1024
INNER = HEADS * HEAD
FF = 2048
CHANNELS = 64
epsilon = 1e-05
masked_score = -2e30
lowest = -1e30
POWER = HEAD**-0.5 * 1.4426950408889634
bf16 = jnp.bfloat16
f32 = jnp.float32

XL, Y, Z = 2, 4, 8
PLANES = XL * Y
TOKENS = 192
PIECE = TOKENS // 2
ROWS = PLANES * PIECE
TILE = 2 * TOKENS
TILES = 2 * ROWS // TILE
HALF = ROWS // 2
BLOCKS = HALF // HEAD
TALL = HEAD + 16
SENT = CHANNELS + 16


def layer_norm(values):
    mean = jnp.mean(values, axis=-1, keepdims=True)
    centred = values - mean
    spread = jnp.mean(centred * centred, axis=-1, keepdims=True)
    return centred * lax.rsqrt(spread + epsilon)


def vmem():
    return pl.BlockSpec(memory_space=pltpu.VMEM)


def smem():
    return pl.BlockSpec(memory_space=pltpu.SMEM)


def anywhere():
    return pl.BlockSpec(memory_space=pl.ANY)


def params(mebibytes):
    return pltpu.CompilerParams(vmem_limit_bytes=mebibytes << 20)


def qkv_kernel(place, hidden, other, w_query, w_key, w_value, slots, weights, normed, sems):
    core = place[0]
    sources = (w_key, w_value, w_query)
    copies = []
    for index, source in enumerate(sources):
        for part in range(2):
            rows = pl.ds(part * (WIDTH // 2), WIDTH // 2)
            copies.append(
                pltpu.make_async_copy(
                    source.at[rows], weights.at[index, rows], sems.at[2 * index + part]
                )
            )
    for copy in copies:
        copy.start()
    rows = pl.ds(pl.multiple_of(core * PIECE, PIECE), PIECE)
    normed[:PIECE, :] = layer_norm(hidden[rows, :].astype(f32)).astype(bf16)
    normed[PIECE:, :] = layer_norm(other[rows, :].astype(f32)).astype(bf16)
    for index, column in enumerate((1, 2, 0)):
        copies[2 * index].wait()
        copies[2 * index + 1].wait()
        made = jnp.dot(normed[...], weights[index], preferred_element_type=f32).astype(bf16)
        for part in range(2):
            sequence = core if part == 0 else 1 - core
            for head in range(HEADS):
                slots[sequence * HEADS + head, :, column * HEAD : (column + 1) * HEAD] = made[
                    part * PIECE : (part + 1) * PIECE, head * HEAD : (head + 1) * HEAD
                ]


def pack_kernel(slots, low, high, queries):
    for part, out in enumerate((low, high)):
        first = part * (PLANES // 2)
        values = []
        for plane in range(PLANES // 2):
            out[plane * PIECE : (plane + 1) * PIECE, :] = slots[first + plane, :, HEAD : 2 * HEAD]
            values.append(slots[first + plane, :, 2 * HEAD :])
        values = jnp.concatenate(values, axis=0)
        for block in range(BLOCKS):
            square = values[block * HEAD : (block + 1) * HEAD, :].astype(f32)
            out[HALF + block * HEAD : HALF + (block + 1) * HEAD, :] = square.T.astype(bf16)
    queries[...] = slots[:, :, :HEAD]


def attend_kernel(parts, sources, first, last, *refs):
    refs = list(refs)
    place = refs.pop(0)
    if first:
        own, other = refs.pop(0), refs.pop(0)
    else:
        queries = refs.pop(0)
    segments = [refs.pop(0) for _ in parts]
    if not first:
        top_in, numer_in = refs.pop(0), refs.pop(0)
    if first:
        queries = refs.pop(0)
        for tile in range(TILES):
            planes = (2 * tile, 2 * tile + 1)
            rows = [own[plane] for plane in planes] + [other[plane] for plane in planes]
            turned = jnp.concatenate(rows, axis=0).astype(f32).T
            queries[:, tile * TILE : (tile + 1) * TILE] = turned.astype(bf16)
    core = place[0]
    column = lax.broadcasted_iota(jnp.int32, (1, TILE), 1)
    column_half = jnp.where(column < TOKENS, core, 1 - core)
    column_plane = (column % TOKENS) // PIECE
    column_place = column_plane * (Z * TOKENS) + column_half * PIECE + column % PIECE
    key = lax.broadcasted_iota(jnp.int32, (HALF, 1), 0)
    key_place = (key // PIECE) * (Z * TOKENS) + key % PIECE + core * PIECE
    ones = jnp.ones((TALL - HEAD, HALF), bf16)
    values = []
    for segment in segments:
        blocks = [segment[HALF + index * HEAD : HALF + (index + 1) * HEAD, :] for index in range(BLOCKS)]
        values.append(jnp.concatenate([jnp.concatenate(blocks, axis=1), ones], axis=0))

    def score(tile):
        columns = slice(tile * TILE, (tile + 1) * TILE)
        found = []
        for segment, part, source, value in zip(segments, parts, sources, values):
            groups = min(2, tile + 1 - 2 * part)
            if groups <= 0:
                continue
            count = groups * TOKENS
            product = jnp.dot(segment[:count, :], queries[:, columns], preferred_element_type=f32)
            if 2 * part + groups - 1 == tile:
                shift = place[1 + source] * TOKENS
                offset = 2 * (tile - 2 * part) * (Z * TOKENS)
                allowed = key_place[:count] + shift <= column_place + offset
                product = jnp.where(allowed, product, masked_score)
            found.append((value[:, :count], product))
        return found

    def finish(tile, found):
        columns = slice(tile * TILE, (tile + 1) * TILE)
        top = jnp.full((1, TILE), lowest, f32) if first else top_in[:1, columns]
        new_top = top
        for _, product in found:
            new_top = jnp.maximum(new_top, jnp.max(product, axis=0, keepdims=True))
        if first:
            sums = jnp.zeros((TALL, TILE), f32)
        else:
            sums = numer_in[:, columns] * jnp.exp2((top - new_top) * POWER)
        for value, product in found:
            weights = jnp.exp2((product - new_top) * POWER).astype(bf16)
            sums = sums + jnp.dot(value, weights, preferred_element_type=f32)
        if not last:
            top_out, numer_out = refs
            top_out[:, columns] = jnp.broadcast_to(new_top, (8, TILE))
            numer_out[:, columns] = sums
            return
        total = sums[HEAD : HEAD + 1, :]
        some = total > 0
        total = jnp.where(some, total, 1.0)
        mixed = (sums[:HEAD, :] / total).T
        level = jnp.where(some, new_top * POWER + jnp.log2(total), lowest)
        level = jnp.broadcast_to(level, (HEAD, TILE)).T
        high = level.astype(bf16)
        rest = level - high.astype(f32)
        middle = rest.astype(bf16)
        low = (rest - middle.astype(f32)).astype(bf16)
        lane = lax.broadcasted_iota(jnp.int32, (TILE, HEAD), 1)
        level = jnp.where(lane == 0, high, jnp.where(lane == 1, middle, low))
        for side in range(2):
            for plane in range(2):
                start = side * TOKENS + plane * PIECE
                refs[side][2 * tile + plane, :, :HEAD] = mixed[start : start + PIECE].astype(bf16)
                refs[side][2 * tile + plane, :, HEAD:] = level[start : start + PIECE]

    found = score(0)
    for tile in range(TILES):
        following = score(tile + 1) if tile + 1 < TILES else None
        finish(tile, found)
        found = following


def attend(place, queries, segments, parts, sources, state, last):
    first = state is None
    stats = [jax.ShapeDtypeStruct((8, 2 * ROWS), f32), jax.ShapeDtypeStruct((TALL, 2 * ROWS), f32)]
    if last:
        shapes = [jax.ShapeDtypeStruct((PLANES, PIECE, 2 * HEAD), bf16)] * 2
    elif first:
        shapes = [jax.ShapeDtypeStruct((HEAD, 2 * ROWS), bf16), *stats]
    else:
        shapes = stats
    operands = [place, *queries, *segments, *(state or ())]
    return pl.pallas_call(
        functools.partial(attend_kernel, parts, sources, first, last),
        out_shape=shapes,
        in_specs=[smem()] + [vmem()] * (len(operands) - 1),
        out_specs=[vmem()] * len(shapes),
        compiler_params=params(24),
        cost_estimate=pl.CostEstimate(
            flops=2 * 2 * 2 * ROWS * HALF * HEAD * len(parts),
            bytes_accessed=3_000_000,
            transcendentals=ROWS * HALF * len(parts),
        ),
    )(*operands)


def merge_kernel(mine, theirs, out):
    def level(block):
        parts = [block[:, :, HEAD + index : HEAD + index + 1].astype(f32) for index in range(3)]
        return parts[0] + parts[1] + parts[2]

    first, second = level(mine), level(theirs)
    top = jnp.maximum(first, second)
    first, second = jnp.exp2(first - top), jnp.exp2(second - top)
    share = 1.0 / (first + second)
    out[...] = (
        (first * share) * mine[:, :, :HEAD].astype(f32)
        + (second * share) * theirs[:, :, :HEAD].astype(f32)
    ).astype(bf16)


FF_PARTS = 4
FF_PART = FF // FF_PARTS


def dense_kernel(
    place,
    attended,
    hidden,
    other,
    flow,
    other_flow,
    w_output,
    w_up,
    w_down,
    w_shift,
    w_scale,
    sent_own,
    sent_other,
    output,
    up,
    down,
    shift_scale,
    sems,
):
    core = place[0]
    copies = [pltpu.make_async_copy(w_output, output, sems.at[0])]
    for part in range(FF_PARTS):
        cut = pl.ds(part * FF_PART, FF_PART)
        copies.append(
            pltpu.make_async_copy(w_up.at[:, cut], up.at[:, cut], sems.at[1 + 2 * part])
        )
        copies.append(pltpu.make_async_copy(w_down.at[cut], down.at[cut], sems.at[2 + 2 * part]))
    for index, source in enumerate((w_shift, w_scale)):
        cut = pl.ds(index * CHANNELS, CHANNELS)
        copies.append(
            pltpu.make_async_copy(source, shift_scale.at[cut], sems.at[1 + 2 * FF_PARTS + index])
        )
    for copy in copies:
        copy.start()
    rows = pl.ds(pl.multiple_of(core * PIECE, PIECE), PIECE)
    residual = jnp.concatenate([hidden[rows, :], other[rows, :]], axis=0).astype(f32)
    sides = []
    for sequence in (core, 1 - core):
        heads = [attended[sequence * HEADS + head] for head in range(HEADS)]
        sides.append(jnp.concatenate(heads, axis=1))
    mixed = jnp.concatenate(sides, axis=0)
    copies[0].wait()
    first = residual + jnp.dot(mixed, output[...], preferred_element_type=f32)
    inner = layer_norm(first).astype(bf16)
    second = first
    for part in range(FF_PARTS):
        cut = slice(part * FF_PART, (part + 1) * FF_PART)
        copies[1 + 2 * part].wait()
        expanded = jnp.dot(inner, up[:, cut], preferred_element_type=f32)
        expanded = jax.nn.gelu(expanded).astype(bf16)
        copies[2 + 2 * part].wait()
        second = second + jnp.dot(expanded, down[cut, :], preferred_element_type=f32)
    features = layer_norm(second).astype(bf16)
    copies[-2].wait()
    copies[-1].wait()
    both = lax.dot_general(
        shift_scale[...], features, (((1,), (1,)), ((), ())), preferred_element_type=f32
    )
    shift, log_scale = both[:CHANNELS], both[CHANNELS:]
    determinant = -jnp.sum(log_scale, axis=0, keepdims=True)
    high = determinant.astype(bf16)
    low = (determinant - high.astype(f32)).astype(bf16)
    row = lax.broadcasted_iota(jnp.int32, (SENT - CHANNELS, TOKENS), 0)
    tail = jnp.where(row == 0, high.astype(f32), jnp.where(row == 1, low.astype(f32), 0.0))
    flows = []
    for source in (flow, other_flow):
        flows.append(jnp.where(core == 0, source[:, :PIECE].astype(f32), source[:, PIECE:].astype(f32)))
    moved = (jnp.concatenate(flows, axis=1) - shift) * jnp.exp(-log_scale)
    sent = jnp.concatenate([moved, tail], axis=0).astype(bf16)
    sent_own[...] = sent[:, :PIECE]
    sent_other[...] = sent[:, PIECE:]


def join_kernel(place, mine, theirs, out):
    core = place[0]
    row = lax.broadcasted_iota(jnp.int32, (PIECE, TOKENS), 0)
    column = lax.broadcasted_iota(jnp.int32, (PIECE, TOKENS), 1)
    total = None
    for source, half in ((mine, core), (theirs, 1 - core)):
        chosen = (column == TOKENS - 1 - half * PIECE - row).astype(f32).astype(bf16)
        term = jnp.dot(source[...], chosen, preferred_element_type=f32)
        total = term if total is None else total + term
    out[...] = total.astype(bf16)


def shift_by(count, step):
    return [(index, (index + step) % count) for index in range(count)]


def on_device(
    hidden, flow_input, w_query, w_key, w_value, w_output, w_up, w_down, w_shift, w_scale
):
    core = lax.axis_index("core")
    z = lax.axis_index("z")
    up_steps = [(z - step) % Z - z for step in range(5)]
    down_steps = [(z + step) % Z - z for step in range(4)]
    place = jnp.stack([core, *up_steps, *down_steps]).astype(jnp.int32)
    other_core = shift_by(2, 1)
    other = lax.ppermute(hidden, "core", other_core)
    other_flow = lax.ppermute(flow_input, "core", other_core)

    slots = pl.pallas_call(
        qkv_kernel,
        out_shape=jax.ShapeDtypeStruct((PLANES, PIECE, 3 * HEAD), bf16),
        in_specs=[smem()] + [vmem()] * 2 + [anywhere()] * 3,
        out_specs=vmem(),
        scratch_shapes=[
            pltpu.VMEM((3, WIDTH, INNER), bf16),
            pltpu.VMEM((TOKENS, WIDTH), bf16),
            pltpu.SemaphoreType.DMA((6,)),
        ],
        compiler_params=params(16),
    )(place, hidden, other, w_query, w_key, w_value)
    slots = lax.all_to_all(slots, ("xl", "y"), 0, 0, tiled=True)
    part = jax.ShapeDtypeStruct((ROWS, HEAD), bf16)
    *own_parts, own_queries = pl.pallas_call(
        pack_kernel,
        out_shape=[part, part, jax.ShapeDtypeStruct((PLANES, PIECE, HEAD), bf16)],
        in_specs=[vmem()],
        out_specs=[vmem()] * 3,
        compiler_params=params(8),
    )(slots)
    other_queries = lax.ppermute(own_queries, "core", other_core)

    up, down = list(own_parts), list(own_parts)
    queries, *state = attend(
        place, (own_queries, other_queries), own_parts, (0, 1), (0, 0), None, False
    )
    for step in range(1, 4):
        for part in range(2):
            up[part] = lax.ppermute(up[part], "z", shift_by(Z, 1))
            down[part] = lax.ppermute(down[part], "z", shift_by(Z, -1))
        state = attend(
            place,
            (queries,),
            up + down,
            (0, 1, 0, 1),
            (step, step, 5 + step, 5 + step),
            state,
            False,
        )
    far = [
        lax.ppermute(up[0], "z", shift_by(Z, 1)),
        lax.ppermute(down[1], "z", shift_by(Z, -1)),
    ]
    mine, others = attend(place, (queries,), far, (0, 1), (4, 4), state, True)
    theirs = lax.ppermute(others, "core", other_core)
    attended = pl.pallas_call(
        merge_kernel,
        out_shape=jax.ShapeDtypeStruct((PLANES, PIECE, HEAD), bf16),
        in_specs=[vmem()] * 2,
        out_specs=vmem(),
        compiler_params=params(8),
    )(mine, theirs)
    attended = lax.all_to_all(attended, ("xl", "y"), 0, 0, tiled=True)

    sent = jax.ShapeDtypeStruct((SENT, PIECE), bf16)
    sent_own, sent_other = pl.pallas_call(
        dense_kernel,
        out_shape=[sent, sent],
        in_specs=[smem()] + [vmem()] * 5 + [anywhere()] * 5,
        out_specs=[vmem()] * 2,
        scratch_shapes=[
            pltpu.VMEM((INNER, WIDTH), bf16),
            pltpu.VMEM((WIDTH, FF), bf16),
            pltpu.VMEM((FF, WIDTH), bf16),
            pltpu.VMEM((2 * CHANNELS, WIDTH), bf16),
            pltpu.SemaphoreType.DMA((3 + 2 * FF_PARTS,)),
        ],
        compiler_params=params(32),
    )(
        place,
        attended,
        hidden,
        other,
        flow_input,
        other_flow,
        w_output,
        w_up,
        w_down,
        w_shift,
        w_scale,
    )
    received = lax.ppermute(sent_other, "core", other_core)
    block = pl.pallas_call(
        join_kernel,
        out_shape=jax.ShapeDtypeStruct((SENT, TOKENS), bf16),
        in_specs=[smem()] + [vmem()] * 2,
        out_specs=vmem(),
        compiler_params=params(8),
    )(place, sent_own, received)
    count = XL * Y * Z
    mirrored = [(index, count - 1 - index) for index in range(count)]
    arrived = lax.ppermute(block, ("xl", "y", "z"), mirrored).astype(f32)
    return (arrived[:CHANNELS], arrived[CHANNELS] + arrived[CHANNELS + 1])


def solution(mesh):
    parts = Mesh(mesh.devices.reshape(2, 2, XL, Y, Z), ("xh", "core", "xl", "y", "z"))
    everywhere = ("xh", "core", "xl", "y", "z")
    in_specs = (P(everywhere, None), P(None, everywhere)) + (P(),) * 8
    out_specs = (P(None, everywhere), P(everywhere))
    return jax.shard_map(
        on_device, mesh=parts, in_specs=in_specs, out_specs=out_specs, check_vma=False
    )
```

```python
import functools

import jax
import jax.numpy as jnp
from jax import lax
from jax.experimental import pallas as pl
from jax.experimental.pallas import tpu as pltpu
from jax.sharding import Mesh, PartitionSpec as P

HEADS = 4
HEAD = 128
WIDTH = 1024
INNER = HEADS * HEAD
FF = 2048
CHANNELS = 64
epsilon = 1e-05
masked_score = -2e30
lowest = -1e30
POWER = HEAD**-0.5 * 1.4426950408889634
bf16 = jnp.bfloat16
f32 = jnp.float32

XL, Y, Z = 2, 4, 8
PLANES = XL * Y
TOKENS = 192
PIECE = TOKENS // 2
ROWS = PLANES * PIECE
TILE = 2 * TOKENS
TILES = 2 * ROWS // TILE
HALF = ROWS // 2
BLOCKS = HALF // HEAD
TALL = HEAD + 16
SENT = CHANNELS + 16


def layer_norm(values):
    mean = jnp.mean(values, axis=-1, keepdims=True)
    centred = values - mean
    spread = jnp.mean(centred * centred, axis=-1, keepdims=True)
    return centred * lax.rsqrt(spread + epsilon)


def vmem():
    return pl.BlockSpec(memory_space=pltpu.VMEM)


def smem():
    return pl.BlockSpec(memory_space=pltpu.SMEM)


def params(mebibytes):
    return pltpu.CompilerParams(vmem_limit_bytes=mebibytes << 20)


def in_hbm(array):
    return pltpu.with_memory_space_constraint(array, pltpu.HBM)


def hbm():
    return pl.BlockSpec(memory_space=pltpu.HBM)


def start_loads(sources, targets, sems):
    copies = []
    for source, target in zip(sources, targets):
        pieces = 4 if source.shape[0] >= 512 else 1
        size = source.shape[0] // pieces
        for piece in range(pieces):
            cut = pl.ds(piece * size, size)
            copies.append(
                pltpu.make_async_copy(source.at[cut], target.at[cut], sems.at[len(copies)])
            )
    for copy in copies:
        copy.start()
    return copies


def load_kernel(place, hidden, w_query, w_key, w_value, own, query, key, value, sems, own_sem):
    rows = pl.ds(pl.multiple_of(place[0] * PIECE, PIECE), PIECE)
    copy = pltpu.make_async_copy(hidden.at[rows], own, own_sem)
    copy.start()
    copies = start_loads((w_key, w_value, w_query), (key, value, query), sems)
    copy.wait()
    for copy in copies:
        copy.wait()


def qkv_kernel(place, own, other, w_query, w_key, w_value, slots, normed):
    core = place[0]
    normed[:PIECE, :] = layer_norm(own[...].astype(f32)).astype(bf16)
    rows = pl.ds(pl.multiple_of(core * PIECE, PIECE), PIECE)
    normed[PIECE:, :] = layer_norm(other[rows, :].astype(f32)).astype(bf16)
    for column, weight in enumerate((w_query, w_key, w_value)):
        made = jnp.dot(normed[...], weight[...], preferred_element_type=f32).astype(bf16)
        for part in range(2):
            sequence = core if part == 0 else 1 - core
            for head in range(HEADS):
                slots[sequence * HEADS + head, :, column * HEAD : (column + 1) * HEAD] = made[
                    part * PIECE : (part + 1) * PIECE, head * HEAD : (head + 1) * HEAD
                ]


def pack_kernel(slots, low, high, queries):
    for part, out in enumerate((low, high)):
        first = part * (PLANES // 2)
        values = []
        for plane in range(PLANES // 2):
            out[plane * PIECE : (plane + 1) * PIECE, :] = slots[first + plane, :, HEAD : 2 * HEAD]
            values.append(slots[first + plane, :, 2 * HEAD :])
        values = jnp.concatenate(values, axis=0)
        for block in range(BLOCKS):
            square = values[block * HEAD : (block + 1) * HEAD, :].astype(f32)
            out[HALF + block * HEAD : HALF + (block + 1) * HEAD, :] = square.T.astype(bf16)
    queries[...] = slots[:, :, :HEAD]


def attend_kernel(parts, sources, first, last, load_count, *refs):
    refs = list(refs)
    place = refs.pop(0)
    if first:
        own, other = refs.pop(0), refs.pop(0)
    else:
        queries = refs.pop(0)
    segments = [refs.pop(0) for _ in parts]
    if not first:
        top_in, numer_in = refs.pop(0), refs.pop(0)
    loads = []
    if load_count:
        weights_in = [refs.pop(0) for _ in range(load_count)]
        sems = refs.pop()
        weights_out = [refs.pop() for _ in range(load_count)][::-1]
        loads = start_loads(weights_in, weights_out, sems)
    if first:
        queries = refs.pop(0)
        for tile in range(TILES):
            planes = (2 * tile, 2 * tile + 1)
            rows = [own[plane] for plane in planes] + [other[plane] for plane in planes]
            turned = jnp.concatenate(rows, axis=0).astype(f32).T
            queries[:, tile * TILE : (tile + 1) * TILE] = turned.astype(bf16)
    core = place[0]
    column = lax.broadcasted_iota(jnp.int32, (1, TILE), 1)
    column_half = jnp.where(column < TOKENS, core, 1 - core)
    column_plane = (column % TOKENS) // PIECE
    column_place = column_plane * (Z * TOKENS) + column_half * PIECE + column % PIECE
    key = lax.broadcasted_iota(jnp.int32, (HALF, 1), 0)
    key_place = (key // PIECE) * (Z * TOKENS) + key % PIECE + core * PIECE
    ones = jnp.ones((TALL - HEAD, HALF), bf16)
    values = []
    for segment in segments:
        blocks = [segment[HALF + index * HEAD : HALF + (index + 1) * HEAD, :] for index in range(BLOCKS)]
        values.append(jnp.concatenate([jnp.concatenate(blocks, axis=1), ones], axis=0))

    def score(tile):
        columns = slice(tile * TILE, (tile + 1) * TILE)
        found = []
        for segment, part, source, value in zip(segments, parts, sources, values):
            groups = min(2, tile + 1 - 2 * part)
            if groups <= 0:
                continue
            count = groups * TOKENS
            product = jnp.dot(segment[:count, :], queries[:, columns], preferred_element_type=f32)
            if 2 * part + groups - 1 == tile:
                shift = place[1 + source] * TOKENS
                offset = 2 * (tile - 2 * part) * (Z * TOKENS)
                allowed = key_place[:count] + shift <= column_place + offset
                product = jnp.where(allowed, product, masked_score)
            found.append((value[:, :count], product))
        return found

    def finish(tile, found):
        columns = slice(tile * TILE, (tile + 1) * TILE)
        top = jnp.full((1, TILE), lowest, f32) if first else top_in[:1, columns]
        new_top = top
        for _, product in found:
            new_top = jnp.maximum(new_top, jnp.max(product, axis=0, keepdims=True))
        if first:
            sums = jnp.zeros((TALL, TILE), f32)
        else:
            sums = numer_in[:, columns] * jnp.exp2((top - new_top) * POWER)
        for value, product in found:
            weights = jnp.exp2((product - new_top) * POWER).astype(bf16)
            sums = sums + jnp.dot(value, weights, preferred_element_type=f32)
        if not last:
            top_out, numer_out = refs
            top_out[:, columns] = jnp.broadcast_to(new_top, (8, TILE))
            numer_out[:, columns] = sums
            return
        total = sums[HEAD : HEAD + 1, :]
        some = total > 0
        total = jnp.where(some, total, 1.0)
        mixed = (sums[:HEAD, :] / total).T
        level = jnp.where(some, new_top * POWER + jnp.log2(total), lowest)
        level = jnp.broadcast_to(level, (HEAD, TILE)).T
        high = level.astype(bf16)
        rest = level - high.astype(f32)
        middle = rest.astype(bf16)
        low = (rest - middle.astype(f32)).astype(bf16)
        lane = lax.broadcasted_iota(jnp.int32, (TILE, HEAD), 1)
        level = jnp.where(lane == 0, high, jnp.where(lane == 1, middle, low))
        for side in range(2):
            for plane in range(2):
                start = side * TOKENS + plane * PIECE
                refs[side][2 * tile + plane, :, :HEAD] = mixed[start : start + PIECE].astype(bf16)
                refs[side][2 * tile + plane, :, HEAD:] = level[start : start + PIECE]

    found = score(0)
    for tile in range(TILES):
        following = score(tile + 1) if tile + 1 < TILES else None
        finish(tile, found)
        found = following
    for load in loads:
        load.wait()


def attend(place, queries, segments, parts, sources, state, last, loads=()):
    first = state is None
    stats = [jax.ShapeDtypeStruct((8, 2 * ROWS), f32), jax.ShapeDtypeStruct((TALL, 2 * ROWS), f32)]
    if last:
        shapes = [jax.ShapeDtypeStruct((PLANES, PIECE, 2 * HEAD), bf16)] * 2
    elif first:
        shapes = [jax.ShapeDtypeStruct((HEAD, 2 * ROWS), bf16), *stats]
    else:
        shapes = stats
    operands = [place, *queries, *segments, *(state or ())]
    in_specs = [smem()] + [vmem()] * (len(operands) - 1) + [hbm()] * len(loads)
    shapes = list(shapes) + [pltpu.VMEM(load.shape, load.dtype) for load in loads]
    operands += [in_hbm(load) for load in loads]
    return pl.pallas_call(
        functools.partial(attend_kernel, parts, sources, first, last, len(loads)),
        out_shape=shapes,
        in_specs=in_specs,
        out_specs=[vmem()] * len(shapes),
        scratch_shapes=[pltpu.SemaphoreType.DMA((4 * len(loads),))] if loads else [],
        compiler_params=params(24),
        cost_estimate=pl.CostEstimate(
            flops=2 * 2 * 2 * ROWS * HALF * HEAD * len(parts),
            bytes_accessed=3_000_000,
            transcendentals=ROWS * HALF * len(parts),
        ),
    )(*operands)


def merge_kernel(mine, theirs, out):
    row = lax.broadcasted_iota(jnp.int32, (HEAD, HEAD), 0)
    spread = (row < 3).astype(f32).astype(bf16)

    def level(block):
        stats = block[:, :, HEAD:].reshape(ROWS, HEAD)
        return jnp.dot(stats, spread, preferred_element_type=f32)

    first, second = level(mine), level(theirs)
    top = jnp.maximum(first, second)
    first, second = jnp.exp2(first - top), jnp.exp2(second - top)
    both = first * mine[:, :, :HEAD].reshape(ROWS, HEAD).astype(f32)
    both = both + second * theirs[:, :, :HEAD].reshape(ROWS, HEAD).astype(f32)
    out[...] = (both / (first + second)).astype(bf16).reshape(PLANES, PIECE, HEAD)


FF_PARTS = 2
FF_PART = FF // FF_PARTS


def dense_kernel(
    place,
    attended,
    own,
    other,
    flow,
    other_flow,
    w_output,
    w_up,
    w_down,
    w_shift,
    w_scale,
    sent_own,
    sent_other,
):
    core = place[0]
    rows = pl.ds(pl.multiple_of(core * PIECE, PIECE), PIECE)
    residual = jnp.concatenate([own[...], other[rows, :]], axis=0).astype(f32)
    sides = []
    for sequence in (core, 1 - core):
        heads = [attended[sequence * HEADS + head] for head in range(HEADS)]
        sides.append(jnp.concatenate(heads, axis=1))
    mixed = jnp.concatenate(sides, axis=0)
    first = residual + jnp.dot(mixed, w_output[...], preferred_element_type=f32)
    inner = layer_norm(first).astype(bf16)
    second = first
    for part in range(FF_PARTS):
        cut = slice(part * FF_PART, (part + 1) * FF_PART)
        expanded = jnp.dot(inner, w_up[:, cut], preferred_element_type=f32)
        expanded = jax.nn.gelu(expanded).astype(bf16)
        second = second + jnp.dot(expanded, w_down[cut, :], preferred_element_type=f32)
    features = layer_norm(second).astype(bf16)
    shift, log_scale = (
        lax.dot_general(
            weight[...], features, (((1,), (1,)), ((), ())), preferred_element_type=f32
        )
        for weight in (w_shift, w_scale)
    )
    determinant = -jnp.sum(log_scale, axis=0, keepdims=True)
    high = determinant.astype(bf16)
    low = (determinant - high.astype(f32)).astype(bf16)
    row = lax.broadcasted_iota(jnp.int32, (SENT - CHANNELS, TOKENS), 0)
    tail = jnp.where(row == 0, high.astype(f32), jnp.where(row == 1, low.astype(f32), 0.0))
    flows = []
    for source in (flow, other_flow):
        flows.append(jnp.where(core == 0, source[:, :PIECE].astype(f32), source[:, PIECE:].astype(f32)))
    moved = (jnp.concatenate(flows, axis=1) - shift) * jnp.exp(-log_scale)
    sent = jnp.concatenate([moved, tail], axis=0).astype(bf16)
    sent_own[...] = sent[:, :PIECE]
    sent_other[...] = sent[:, PIECE:]


def join_kernel(place, mine, theirs, out):
    core = place[0]
    row = lax.broadcasted_iota(jnp.int32, (PIECE, TOKENS), 0)
    column = lax.broadcasted_iota(jnp.int32, (PIECE, TOKENS), 1)
    total = None
    for source, half in ((mine, core), (theirs, 1 - core)):
        chosen = (column == TOKENS - 1 - half * PIECE - row).astype(f32).astype(bf16)
        term = jnp.dot(source[...], chosen, preferred_element_type=f32)
        total = term if total is None else total + term
    out[...] = total.astype(bf16)


def shift_by(count, step):
    return [(index, (index + step) % count) for index in range(count)]


def on_device(
    hidden, flow_input, w_query, w_key, w_value, w_output, w_up, w_down, w_shift, w_scale
):
    core = lax.axis_index("core")
    z = lax.axis_index("z")
    up_steps = [(z - step) % Z - z for step in range(5)]
    down_steps = [(z + step) % Z - z for step in range(4)]
    place = jnp.stack([core, *up_steps, *down_steps]).astype(jnp.int32)
    other_core = shift_by(2, 1)
    other = lax.ppermute(hidden, "core", other_core)
    other_flow = lax.ppermute(flow_input, "core", other_core)

    square = pltpu.VMEM((WIDTH, INNER), bf16)
    own, *weights = pl.pallas_call(
        load_kernel,
        out_shape=[pltpu.VMEM((PIECE, WIDTH), bf16), square, square, square],
        in_specs=[smem()] + [hbm()] * 4,
        out_specs=[vmem()] * 4,
        scratch_shapes=[pltpu.SemaphoreType.DMA((12,)), pltpu.SemaphoreType.DMA],
        compiler_params=params(8),
        cost_estimate=pl.CostEstimate(flops=0, bytes_accessed=6_600_000, transcendentals=0),
    )(place, *(in_hbm(array) for array in (hidden, w_query, w_key, w_value)))
    slots = pl.pallas_call(
        qkv_kernel,
        out_shape=jax.ShapeDtypeStruct((PLANES, PIECE, 3 * HEAD), bf16),
        in_specs=[smem()] + [vmem()] * 5,
        out_specs=vmem(),
        scratch_shapes=[pltpu.VMEM((TOKENS, WIDTH), bf16)],
        compiler_params=params(8),
    )(place, own, other, *weights)
    slots = lax.all_to_all(slots, ("xl", "y"), 0, 0, tiled=True)
    part = jax.ShapeDtypeStruct((ROWS, HEAD), bf16)
    *own_parts, own_queries = pl.pallas_call(
        pack_kernel,
        out_shape=[part, part, jax.ShapeDtypeStruct((PLANES, PIECE, HEAD), bf16)],
        in_specs=[vmem()],
        out_specs=[vmem()] * 3,
        compiler_params=params(8),
    )(slots)
    other_queries = lax.ppermute(own_queries, "core", other_core)

    up, down = list(own_parts), list(own_parts)
    queries, *state = attend(
        place, (own_queries, other_queries), own_parts, (0, 1), (0, 0), None, False
    )
    loads = {1: (w_output, w_up), 2: (w_down, w_shift, w_scale), 3: ()}
    dense_weights = []
    for step in range(1, 4):
        for part in range(2):
            up[part] = lax.ppermute(up[part], "z", shift_by(Z, 1))
            down[part] = lax.ppermute(down[part], "z", shift_by(Z, -1))
        state = attend(
            place,
            (queries,),
            up + down,
            (0, 1, 0, 1),
            (step, step, 5 + step, 5 + step),
            state,
            False,
            loads[step],
        )
        dense_weights += state[2:]
        state = state[:2]
    far = [
        lax.ppermute(up[0], "z", shift_by(Z, 1)),
        lax.ppermute(down[1], "z", shift_by(Z, -1)),
    ]
    mine, others = attend(place, (queries,), far, (0, 1), (4, 4), state, True)
    theirs = lax.ppermute(others, "core", other_core)
    attended = pl.pallas_call(
        merge_kernel,
        out_shape=jax.ShapeDtypeStruct((PLANES, PIECE, HEAD), bf16),
        in_specs=[vmem()] * 2,
        out_specs=vmem(),
        compiler_params=params(8),
    )(mine, theirs)
    attended = lax.all_to_all(attended, ("xl", "y"), 0, 0, tiled=True)

    sent = jax.ShapeDtypeStruct((SENT, PIECE), bf16)
    sent_own, sent_other = pl.pallas_call(
        dense_kernel,
        out_shape=[sent, sent],
        in_specs=[smem()] + [vmem()] * 10,
        out_specs=[vmem()] * 2,
        compiler_params=params(16),
    )(place, attended, own, other, flow_input, other_flow, *dense_weights)
    received = lax.ppermute(sent_other, "core", other_core)
    block = pl.pallas_call(
        join_kernel,
        out_shape=jax.ShapeDtypeStruct((SENT, TOKENS), bf16),
        in_specs=[smem()] + [vmem()] * 2,
        out_specs=vmem(),
        compiler_params=params(8),
    )(place, sent_own, received)
    count = XL * Y * Z
    mirrored = [(index, count - 1 - index) for index in range(count)]
    arrived = lax.ppermute(block, ("xl", "y", "z"), mirrored).astype(f32)
    return (arrived[:CHANNELS], arrived[CHANNELS] + arrived[CHANNELS + 1])


def solution(mesh):
    parts = Mesh(mesh.devices.reshape(2, 2, XL, Y, Z), ("xh", "core", "xl", "y", "z"))
    everywhere = ("xh", "core", "xl", "y", "z")
    in_specs = (P(everywhere, None), P(None, everywhere)) + (P(),) * 8
    out_specs = (P(None, everywhere), P(everywhere))
    return jax.shard_map(
        on_device, mesh=parts, in_specs=in_specs, out_specs=out_specs, check_vma=False
    )
```

```python
import functools

import jax
import jax.numpy as jnp
from jax import lax
from jax.experimental import pallas as pl
from jax.experimental.pallas import tpu as pltpu
from jax.sharding import Mesh, PartitionSpec as P

HEADS = 4
HEAD = 128
WIDTH = 1024
INNER = HEADS * HEAD
FF = 2048
CHANNELS = 64
epsilon = 1e-05
masked_score = -2e30
lowest = -1e30
POWER = HEAD**-0.5 * 1.4426950408889634
bf16 = jnp.bfloat16
f32 = jnp.float32

XL, Y, Z = 2, 4, 8
PLANES = XL * Y
TOKENS = 192
PIECE = TOKENS // 2
ROWS = PLANES * PIECE
TILE = 2 * TOKENS
TILES = 2 * ROWS // TILE
HALF = ROWS // 2
BLOCKS = HALF // HEAD
TALL = HEAD + 16
SENT = CHANNELS + 16


def layer_norm(values):
    mean = jnp.mean(values, axis=-1, keepdims=True)
    centred = values - mean
    spread = jnp.mean(centred * centred, axis=-1, keepdims=True)
    return centred * lax.rsqrt(spread + epsilon)


def vmem():
    return pl.BlockSpec(memory_space=pltpu.VMEM)


def smem():
    return pl.BlockSpec(memory_space=pltpu.SMEM)


def params(mebibytes):
    return pltpu.CompilerParams(vmem_limit_bytes=mebibytes << 20)


def in_hbm(array):
    return pltpu.with_memory_space_constraint(array, pltpu.HBM)


def hbm():
    return pl.BlockSpec(memory_space=pltpu.HBM)


def start_loads(sources, targets, sems):
    copies = []
    for source, target in zip(sources, targets):
        pieces = 4 if source.shape[0] >= 512 else 1
        size = source.shape[0] // pieces
        for piece in range(pieces):
            cut = pl.ds(piece * size, size)
            copies.append(
                pltpu.make_async_copy(source.at[cut], target.at[cut], sems.at[len(copies)])
            )
    for copy in copies:
        copy.start()
    return copies


def load_kernel(place, hidden, w_query, w_key, w_value, own, query, key, value, sems, own_sem):
    rows = pl.ds(pl.multiple_of(place[0] * PIECE, PIECE), PIECE)
    copy = pltpu.make_async_copy(hidden.at[rows], own, own_sem)
    copy.start()
    copies = start_loads((w_key, w_value, w_query), (key, value, query), sems)
    copy.wait()
    for copy in copies:
        copy.wait()


def qkv_kernel(place, own, other, w_query, w_key, w_value, slots, normed):
    core = place[0]
    normed[:PIECE, :] = layer_norm(own[...].astype(f32)).astype(bf16)
    rows = pl.ds(pl.multiple_of(core * PIECE, PIECE), PIECE)
    normed[PIECE:, :] = layer_norm(other[rows, :].astype(f32)).astype(bf16)
    for column, weight in enumerate((w_query, w_key, w_value)):
        made = jnp.dot(normed[...], weight[...], preferred_element_type=f32).astype(bf16)
        for part in range(2):
            sequence = core if part == 0 else 1 - core
            for head in range(HEADS):
                slots[sequence * HEADS + head, :, column * HEAD : (column + 1) * HEAD] = made[
                    part * PIECE : (part + 1) * PIECE, head * HEAD : (head + 1) * HEAD
                ]


def pack_kernel(slots, low, high, queries):
    for part, out in enumerate((low, high)):
        first = part * (PLANES // 2)
        values = []
        for plane in range(PLANES // 2):
            out[plane * PIECE : (plane + 1) * PIECE, :] = slots[first + plane, :, HEAD : 2 * HEAD]
            values.append(slots[first + plane, :, 2 * HEAD :])
        values = jnp.concatenate(values, axis=0)
        for block in range(BLOCKS):
            square = values[block * HEAD : (block + 1) * HEAD, :].astype(f32)
            out[HALF + block * HEAD : HALF + (block + 1) * HEAD, :] = square.T.astype(bf16)
    queries[...] = slots[:, :, :HEAD]


def attend_kernel(parts, sources, first, last, after, *refs):
    refs = list(refs)
    place = refs.pop(0)
    if first:
        own, other = refs.pop(0), refs.pop(0)
    else:
        queries = refs.pop(0)
    segments = [refs.pop(0) for _ in parts]
    if not first:
        top_in, numer_in = refs.pop(0), refs.pop(0)
    refs = refs[after:]
    if first:
        queries = refs.pop(0)
        for tile in range(TILES):
            planes = (2 * tile, 2 * tile + 1)
            rows = [own[plane] for plane in planes] + [other[plane] for plane in planes]
            turned = jnp.concatenate(rows, axis=0).astype(f32).T
            queries[:, tile * TILE : (tile + 1) * TILE] = turned.astype(bf16)
    core = place[0]
    column = lax.broadcasted_iota(jnp.int32, (1, TILE), 1)
    column_half = jnp.where(column < TOKENS, core, 1 - core)
    column_plane = (column % TOKENS) // PIECE
    column_place = column_plane * (Z * TOKENS) + column_half * PIECE + column % PIECE
    key = lax.broadcasted_iota(jnp.int32, (HALF, 1), 0)
    key_place = (key // PIECE) * (Z * TOKENS) + key % PIECE + core * PIECE
    ones = jnp.ones((TALL - HEAD, HALF), bf16)
    values = []
    for segment in segments:
        blocks = [segment[HALF + index * HEAD : HALF + (index + 1) * HEAD, :] for index in range(BLOCKS)]
        values.append(jnp.concatenate([jnp.concatenate(blocks, axis=1), ones], axis=0))

    def score(tile):
        columns = slice(tile * TILE, (tile + 1) * TILE)
        found = []
        for segment, part, source, value in zip(segments, parts, sources, values):
            groups = min(2, tile + 1 - 2 * part)
            if groups <= 0:
                continue
            count = groups * TOKENS
            product = jnp.dot(segment[:count, :], queries[:, columns], preferred_element_type=f32)
            if 2 * part + groups - 1 == tile:
                shift = place[1 + source] * TOKENS
                offset = 2 * (tile - 2 * part) * (Z * TOKENS)
                allowed = key_place[:count] + shift <= column_place + offset
                product = jnp.where(allowed, product, masked_score)
            found.append((value[:, :count], product))
        return found

    def finish(tile, found):
        columns = slice(tile * TILE, (tile + 1) * TILE)
        top = jnp.full((1, TILE), lowest, f32) if first else top_in[:1, columns]
        new_top = top
        for _, product in found:
            new_top = jnp.maximum(new_top, jnp.max(product, axis=0, keepdims=True))
        if first:
            sums = jnp.zeros((TALL, TILE), f32)
        else:
            sums = numer_in[:, columns] * jnp.exp2((top - new_top) * POWER)
        for value, product in found:
            weights = jnp.exp2((product - new_top) * POWER).astype(bf16)
            sums = sums + jnp.dot(value, weights, preferred_element_type=f32)
        if not last:
            top_out, numer_out = refs
            top_out[:, columns] = jnp.broadcast_to(new_top, (8, TILE))
            numer_out[:, columns] = sums
            return
        total = sums[HEAD : HEAD + 1, :]
        some = total > 0
        total = jnp.where(some, total, 1.0)
        mixed = (sums[:HEAD, :] / total).T
        level = jnp.where(some, new_top * POWER + jnp.log2(total), lowest)
        level = jnp.broadcast_to(level, (HEAD, TILE)).T
        high = level.astype(bf16)
        rest = level - high.astype(f32)
        middle = rest.astype(bf16)
        low = (rest - middle.astype(f32)).astype(bf16)
        lane = lax.broadcasted_iota(jnp.int32, (TILE, HEAD), 1)
        level = jnp.where(lane == 0, high, jnp.where(lane == 1, middle, low))
        for side in range(2):
            for plane in range(2):
                start = side * TOKENS + plane * PIECE
                refs[side][2 * tile + plane, :, :HEAD] = mixed[start : start + PIECE].astype(bf16)
                refs[side][2 * tile + plane, :, HEAD:] = level[start : start + PIECE]

    found = score(0)
    for tile in range(TILES):
        following = score(tile + 1) if tile + 1 < TILES else None
        finish(tile, found)
        found = following


def attend(place, queries, segments, parts, sources, state, last, after=()):
    first = state is None
    stats = [jax.ShapeDtypeStruct((8, 2 * ROWS), f32), jax.ShapeDtypeStruct((TALL, 2 * ROWS), f32)]
    if last:
        shapes = [jax.ShapeDtypeStruct((PLANES, PIECE, 2 * HEAD), bf16)] * 2
    elif first:
        shapes = [jax.ShapeDtypeStruct((HEAD, 2 * ROWS), bf16), *stats]
    else:
        shapes = stats
    operands = [place, *queries, *segments, *(state or ()), *after]
    return pl.pallas_call(
        functools.partial(attend_kernel, parts, sources, first, last, len(after)),
        out_shape=shapes,
        in_specs=[smem()] + [vmem()] * (len(operands) - 1),
        out_specs=[vmem()] * len(shapes),
        compiler_params=params(16),
        cost_estimate=pl.CostEstimate(
            flops=8 * 2 * 2 * ROWS * HALF * HEAD * len(parts),
            bytes_accessed=3_000_000,
            transcendentals=ROWS * HALF * len(parts),
        ),
    )(*operands)


def merge_kernel(mine, theirs, out):
    row = lax.broadcasted_iota(jnp.int32, (HEAD, HEAD), 0)
    spread = (row < 3).astype(f32).astype(bf16)

    def level(block):
        stats = block[:, :, HEAD:].reshape(ROWS, HEAD)
        return jnp.dot(stats, spread, preferred_element_type=f32)

    first, second = level(mine), level(theirs)
    top = jnp.maximum(first, second)
    first, second = jnp.exp2(first - top), jnp.exp2(second - top)
    both = first * mine[:, :, :HEAD].reshape(ROWS, HEAD).astype(f32)
    both = both + second * theirs[:, :, :HEAD].reshape(ROWS, HEAD).astype(f32)
    out[...] = (both / (first + second)).astype(bf16).reshape(PLANES, PIECE, HEAD)


FF_PARTS = 2
FF_PART = FF // FF_PARTS


def dense_kernel(
    place,
    attended,
    own,
    other,
    flow,
    other_flow,
    w_output,
    w_up,
    w_down,
    w_shift,
    w_scale,
    sent_own,
    sent_other,
):
    core = place[0]
    rows = pl.ds(pl.multiple_of(core * PIECE, PIECE), PIECE)
    residual = jnp.concatenate([own[...], other[rows, :]], axis=0).astype(f32)
    sides = []
    for sequence in (core, 1 - core):
        heads = [attended[sequence * HEADS + head] for head in range(HEADS)]
        sides.append(jnp.concatenate(heads, axis=1))
    mixed = jnp.concatenate(sides, axis=0)
    first = residual + jnp.dot(mixed, w_output[...], preferred_element_type=f32)
    inner = layer_norm(first).astype(bf16)
    second = first
    for part in range(FF_PARTS):
        cut = slice(part * FF_PART, (part + 1) * FF_PART)
        expanded = jnp.dot(inner, w_up[:, cut], preferred_element_type=f32)
        expanded = jax.nn.gelu(expanded).astype(bf16)
        second = second + jnp.dot(expanded, w_down[cut, :], preferred_element_type=f32)
    features = layer_norm(second).astype(bf16)
    shift, log_scale = (
        lax.dot_general(
            weight[...], features, (((1,), (1,)), ((), ())), preferred_element_type=f32
        )
        for weight in (w_shift, w_scale)
    )
    determinant = -jnp.sum(log_scale, axis=0, keepdims=True)
    high = determinant.astype(bf16)
    low = (determinant - high.astype(f32)).astype(bf16)
    row = lax.broadcasted_iota(jnp.int32, (SENT - CHANNELS, TOKENS), 0)
    tail = jnp.where(row == 0, high.astype(f32), jnp.where(row == 1, low.astype(f32), 0.0))
    flows = []
    for source in (flow, other_flow):
        flows.append(jnp.where(core == 0, source[:, :PIECE].astype(f32), source[:, PIECE:].astype(f32)))
    moved = (jnp.concatenate(flows, axis=1) - shift) * jnp.exp(-log_scale)
    sent = jnp.concatenate([moved, tail], axis=0).astype(bf16)
    sent_own[...] = sent[:, :PIECE]
    sent_other[...] = sent[:, PIECE:]


def join_kernel(place, mine, theirs, out):
    core = place[0]
    row = lax.broadcasted_iota(jnp.int32, (PIECE, TOKENS), 0)
    column = lax.broadcasted_iota(jnp.int32, (PIECE, TOKENS), 1)
    total = None
    for source, half in ((mine, core), (theirs, 1 - core)):
        chosen = (column == TOKENS - 1 - half * PIECE - row).astype(f32).astype(bf16)
        term = jnp.dot(source[...], chosen, preferred_element_type=f32)
        total = term if total is None else total + term
    out[...] = total.astype(bf16)


def shift_by(count, step):
    return [(index, (index + step) % count) for index in range(count)]


def on_device(
    hidden, flow_input, w_query, w_key, w_value, w_output, w_up, w_down, w_shift, w_scale
):
    core = lax.axis_index("core")
    z = lax.axis_index("z")
    up_steps = [(z - step) % Z - z for step in range(5)]
    down_steps = [(z + step) % Z - z for step in range(4)]
    place = jnp.stack([core, *up_steps, *down_steps]).astype(jnp.int32)
    other_core = shift_by(2, 1)
    other = lax.ppermute(hidden, "core", other_core)
    other_flow = lax.ppermute(flow_input, "core", other_core)

    square = pltpu.VMEM((WIDTH, INNER), bf16)
    own, *weights = pl.pallas_call(
        load_kernel,
        out_shape=[pltpu.VMEM((PIECE, WIDTH), bf16), square, square, square],
        in_specs=[smem()] + [hbm()] * 4,
        out_specs=[vmem()] * 4,
        scratch_shapes=[pltpu.SemaphoreType.DMA((12,)), pltpu.SemaphoreType.DMA],
        compiler_params=params(8),
        cost_estimate=pl.CostEstimate(flops=0, bytes_accessed=6_600_000, transcendentals=0),
    )(place, *(in_hbm(array) for array in (hidden, w_query, w_key, w_value)))
    slots = pl.pallas_call(
        qkv_kernel,
        out_shape=jax.ShapeDtypeStruct((PLANES, PIECE, 3 * HEAD), bf16),
        in_specs=[smem()] + [vmem()] * 5,
        out_specs=vmem(),
        scratch_shapes=[pltpu.VMEM((TOKENS, WIDTH), bf16)],
        compiler_params=params(8),
    )(place, own, other, *weights)
    slots = lax.all_to_all(slots, ("xl", "y"), 0, 0, tiled=True)
    part = jax.ShapeDtypeStruct((ROWS, HEAD), bf16)
    *own_parts, own_queries = pl.pallas_call(
        pack_kernel,
        out_shape=[part, part, jax.ShapeDtypeStruct((PLANES, PIECE, HEAD), bf16)],
        in_specs=[vmem()],
        out_specs=[vmem()] * 3,
        compiler_params=params(8),
    )(slots)
    other_queries = lax.ppermute(own_queries, "core", other_core)

    up, down = list(own_parts), list(own_parts)
    queries, *state = attend(
        place, (own_queries, other_queries), own_parts, (0, 1), (0, 0), None, False
    )
    for step in range(1, 4):
        for part in range(2):
            up[part] = lax.ppermute(up[part], "z", shift_by(Z, 1))
            down[part] = lax.ppermute(down[part], "z", shift_by(Z, -1))
        state = attend(
            place,
            (queries,),
            up + down,
            (0, 1, 0, 1),
            (step, step, 5 + step, 5 + step),
            state,
            False,
            (other_flow,) if step == 1 else (),
        )
    far = [
        lax.ppermute(up[0], "z", shift_by(Z, 1)),
        lax.ppermute(down[1], "z", shift_by(Z, -1)),
    ]
    mine, others = attend(place, (queries,), far, (0, 1), (4, 4), state, True)
    theirs = lax.ppermute(others, "core", other_core)
    attended = pl.pallas_call(
        merge_kernel,
        out_shape=jax.ShapeDtypeStruct((PLANES, PIECE, HEAD), bf16),
        in_specs=[vmem()] * 2,
        out_specs=vmem(),
        compiler_params=params(8),
    )(mine, theirs)
    attended = lax.all_to_all(attended, ("xl", "y"), 0, 0, tiled=True)

    sent = jax.ShapeDtypeStruct((SENT, PIECE), bf16)
    sent_own, sent_other = pl.pallas_call(
        dense_kernel,
        out_shape=[sent, sent],
        in_specs=[smem()] + [vmem()] * 10,
        out_specs=[vmem()] * 2,
        compiler_params=params(16),
    )(
        place,
        attended,
        own,
        other,
        flow_input,
        other_flow,
        w_output,
        w_up,
        w_down,
        w_shift,
        w_scale,
    )
    received = lax.ppermute(sent_other, "core", other_core)
    block = pl.pallas_call(
        join_kernel,
        out_shape=jax.ShapeDtypeStruct((SENT, TOKENS), bf16),
        in_specs=[smem()] + [vmem()] * 2,
        out_specs=vmem(),
        compiler_params=params(8),
    )(place, sent_own, received)
    count = XL * Y * Z
    mirrored = [(index, count - 1 - index) for index in range(count)]
    arrived = lax.ppermute(block, ("xl", "y", "z"), mirrored).astype(f32)
    return (arrived[:CHANNELS], arrived[CHANNELS] + arrived[CHANNELS + 1])


def solution(mesh):
    parts = Mesh(mesh.devices.reshape(2, 2, XL, Y, Z), ("xh", "core", "xl", "y", "z"))
    everywhere = ("xh", "core", "xl", "y", "z")
    in_specs = (P(everywhere, None), P(None, everywhere)) + (P(),) * 8
    out_specs = (P(None, everywhere), P(everywhere))
    return jax.shard_map(
        on_device, mesh=parts, in_specs=in_specs, out_specs=out_specs, check_vma=False
    )
```

```python
import functools

import jax
import jax.numpy as jnp
from jax import lax
from jax.experimental import pallas as pl
from jax.experimental.pallas import tpu as pltpu
from jax.sharding import Mesh, PartitionSpec as P

HEADS = 4
HEAD = 128
WIDTH = 1024
INNER = HEADS * HEAD
FF = 2048
CHANNELS = 64
epsilon = 1e-05
masked_score = -2e30
lowest = -1e30
POWER = HEAD**-0.5 * 1.4426950408889634
bf16 = jnp.bfloat16
f32 = jnp.float32

XL, Y, Z = 2, 4, 8
PLANES = XL * Y
TOKENS = 192
PIECE = TOKENS // 2
ROWS = PLANES * PIECE
TILE = 2 * TOKENS
TILES = 2 * ROWS // TILE
HALF = ROWS // 2
BLOCKS = HALF // HEAD
FIRST_COST, COST = 4, 32
TALL = HEAD + 16
SENT = CHANNELS + 16


def layer_norm(values):
    mean = jnp.mean(values, axis=-1, keepdims=True)
    centred = values - mean
    spread = jnp.mean(centred * centred, axis=-1, keepdims=True)
    return centred * lax.rsqrt(spread + epsilon)


def vmem():
    return pl.BlockSpec(memory_space=pltpu.VMEM)


def smem():
    return pl.BlockSpec(memory_space=pltpu.SMEM)


def params(mebibytes):
    return pltpu.CompilerParams(vmem_limit_bytes=mebibytes << 20)


def in_hbm(array):
    return pltpu.with_memory_space_constraint(array, pltpu.HBM)


def hbm():
    return pl.BlockSpec(memory_space=pltpu.HBM)


def start_loads(sources, targets, sems):
    copies = []
    for source, target in zip(sources, targets):
        pieces = 4 if source.shape[0] >= 512 else 1
        size = source.shape[0] // pieces
        for piece in range(pieces):
            cut = pl.ds(piece * size, size)
            copies.append(
                pltpu.make_async_copy(source.at[cut], target.at[cut], sems.at[len(copies)])
            )
    for copy in copies:
        copy.start()
    return copies


def load_kernel(place, hidden, w_query, w_key, w_value, own, query, key, value, sems, own_sem):
    rows = pl.ds(pl.multiple_of(place[0] * PIECE, PIECE), PIECE)
    copy = pltpu.make_async_copy(hidden.at[rows], own, own_sem)
    copy.start()
    copies = start_loads((w_key, w_value, w_query), (key, value, query), sems)
    copy.wait()
    for copy in copies:
        copy.wait()


def qkv_kernel(place, own, other, w_query, w_key, w_value, slots, normed):
    core = place[0]
    normed[:PIECE, :] = layer_norm(own[...].astype(f32)).astype(bf16)
    rows = pl.ds(pl.multiple_of(core * PIECE, PIECE), PIECE)
    normed[PIECE:, :] = layer_norm(other[rows, :].astype(f32)).astype(bf16)
    for column, weight in enumerate((w_query, w_key, w_value)):
        made = jnp.dot(normed[...], weight[...], preferred_element_type=f32).astype(bf16)
        for part in range(2):
            sequence = core if part == 0 else 1 - core
            for head in range(HEADS):
                slots[sequence * HEADS + head, :, column * HEAD : (column + 1) * HEAD] = made[
                    part * PIECE : (part + 1) * PIECE, head * HEAD : (head + 1) * HEAD
                ]


def pack_kernel(slots, chunk, queries):
    for part in range(2):
        first = part * (PLANES // 2)
        base = part * ROWS
        values = []
        for plane in range(PLANES // 2):
            start = base + plane * PIECE
            chunk[start : start + PIECE, :] = slots[first + plane, :, HEAD : 2 * HEAD]
            values.append(slots[first + plane, :, 2 * HEAD :])
        values = jnp.concatenate(values, axis=0)
        for block in range(BLOCKS):
            square = values[block * HEAD : (block + 1) * HEAD, :].astype(f32)
            start = base + HALF + block * HEAD
            chunk[start : start + HEAD, :] = square.T.astype(bf16)
    queries[...] = slots[:, :, :HEAD]


def attend_kernel(chunks, first, last, after, *refs):
    refs = list(refs)
    place = refs.pop(0)
    if first:
        own, other = refs.pop(0), refs.pop(0)
    else:
        queries = refs.pop(0)
    segments = []
    for halves, source in chunks:
        chunk = refs.pop(0)
        for index, part in enumerate(halves):
            segments.append((chunk, index * ROWS, part, source))
    if not first:
        top_in, numer_in = refs.pop(0), refs.pop(0)
    refs = refs[after:]
    if first:
        queries = refs.pop(0)
        for tile in range(TILES):
            planes = (2 * tile, 2 * tile + 1)
            rows = [own[plane] for plane in planes] + [other[plane] for plane in planes]
            turned = jnp.concatenate(rows, axis=0).astype(f32).T
            queries[:, tile * TILE : (tile + 1) * TILE] = turned.astype(bf16)
    core = place[0]
    column = lax.broadcasted_iota(jnp.int32, (1, TILE), 1)
    column_half = jnp.where(column < TOKENS, core, 1 - core)
    column_plane = (column % TOKENS) // PIECE
    column_place = column_plane * (Z * TOKENS) + column_half * PIECE + column % PIECE
    key = lax.broadcasted_iota(jnp.int32, (HALF, 1), 0)
    key_place = (key // PIECE) * (Z * TOKENS) + key % PIECE + core * PIECE
    ones = jnp.ones((TALL - HEAD, HALF), bf16)
    values = []
    for chunk, base, _, _ in segments:
        starts = [base + HALF + index * HEAD for index in range(BLOCKS)]
        blocks = [chunk[start : start + HEAD, :] for start in starts]
        values.append(jnp.concatenate([jnp.concatenate(blocks, axis=1), ones], axis=0))

    def score(tile):
        columns = slice(tile * TILE, (tile + 1) * TILE)
        found = []
        for (chunk, base, part, source), value in zip(segments, values):
            groups = min(2, tile + 1 - 2 * part)
            if groups <= 0:
                continue
            count = groups * TOKENS
            product = jnp.dot(
                chunk[base : base + count, :], queries[:, columns], preferred_element_type=f32
            )
            if 2 * part + groups - 1 == tile:
                shift = place[1 + source] * TOKENS
                offset = 2 * (tile - 2 * part) * (Z * TOKENS)
                allowed = key_place[:count] + shift <= column_place + offset
                product = jnp.where(allowed, product, masked_score)
            found.append((value[:, :count], product))
        return found

    def finish(tile, found):
        columns = slice(tile * TILE, (tile + 1) * TILE)
        top = jnp.full((1, TILE), lowest, f32) if first else top_in[:1, columns]
        new_top = top
        for _, product in found:
            new_top = jnp.maximum(new_top, jnp.max(product, axis=0, keepdims=True))
        if first:
            sums = jnp.zeros((TALL, TILE), f32)
        else:
            sums = numer_in[:, columns] * jnp.exp2((top - new_top) * POWER)
        for value, product in found:
            weights = jnp.exp2((product - new_top) * POWER).astype(bf16)
            sums = sums + jnp.dot(value, weights, preferred_element_type=f32)
        if not last:
            top_out, numer_out = refs
            top_out[:, columns] = jnp.broadcast_to(new_top, (8, TILE))
            numer_out[:, columns] = sums
            return
        total = sums[HEAD : HEAD + 1, :]
        some = total > 0
        total = jnp.where(some, total, 1.0)
        mixed = (sums[:HEAD, :] / total).T
        level = jnp.where(some, new_top * POWER + jnp.log2(total), lowest)
        level = jnp.broadcast_to(level, (HEAD, TILE)).T
        high = level.astype(bf16)
        rest = level - high.astype(f32)
        middle = rest.astype(bf16)
        low = (rest - middle.astype(f32)).astype(bf16)
        lane = lax.broadcasted_iota(jnp.int32, (TILE, HEAD), 1)
        level = jnp.where(lane == 0, high, jnp.where(lane == 1, middle, low))
        for side in range(2):
            for plane in range(2):
                start = side * TOKENS + plane * PIECE
                refs[side][2 * tile + plane, :, :HEAD] = mixed[start : start + PIECE].astype(bf16)
                refs[side][2 * tile + plane, :, HEAD:] = level[start : start + PIECE]

    found = score(0)
    for tile in range(TILES):
        following = score(tile + 1) if tile + 1 < TILES else None
        finish(tile, found)
        found = following


def attend(place, queries, segments, chunks, state, last, after=()):
    first = state is None
    count = sum(len(halves) for halves, _ in chunks)
    stats = [jax.ShapeDtypeStruct((8, 2 * ROWS), f32), jax.ShapeDtypeStruct((TALL, 2 * ROWS), f32)]
    if last:
        shapes = [jax.ShapeDtypeStruct((PLANES, PIECE, 2 * HEAD), bf16)] * 2
    elif first:
        shapes = [jax.ShapeDtypeStruct((HEAD, 2 * ROWS), bf16), *stats]
    else:
        shapes = stats
    operands = [place, *queries, *segments, *(state or ()), *after]
    return pl.pallas_call(
        functools.partial(attend_kernel, chunks, first, last, len(after)),
        out_shape=shapes,
        in_specs=[smem()] + [vmem()] * (len(operands) - 1),
        out_specs=[vmem()] * len(shapes),
        compiler_params=params(16),
        cost_estimate=pl.CostEstimate(
            flops=(FIRST_COST if first else COST) * ROWS * HALF * HEAD * count,
            bytes_accessed=3_000_000,
            transcendentals=ROWS * HALF * count,
        ),
    )(*operands)


def merge_kernel(mine, theirs, out):
    row = lax.broadcasted_iota(jnp.int32, (HEAD, HEAD), 0)
    spread = (row < 3).astype(f32).astype(bf16)

    def level(block):
        stats = block[:, :, HEAD:].reshape(ROWS, HEAD)
        return jnp.dot(stats, spread, preferred_element_type=f32)

    first, second = level(mine), level(theirs)
    top = jnp.maximum(first, second)
    first, second = jnp.exp2(first - top), jnp.exp2(second - top)
    both = first * mine[:, :, :HEAD].reshape(ROWS, HEAD).astype(f32)
    both = both + second * theirs[:, :, :HEAD].reshape(ROWS, HEAD).astype(f32)
    both = (both / (first + second)).astype(bf16).reshape(PLANES, PIECE, HEAD)
    for plane in range(PLANES):
        out[PLANES - 1 - plane] = both[plane]


FF_PARTS = 2
FF_PART = FF // FF_PARTS


def dense_kernel(
    place,
    attended,
    hidden,
    other,
    flow,
    other_flow,
    w_output,
    w_up,
    w_down,
    w_shift,
    w_scale,
    sent_own,
    sent_other,
):
    core = place[0]
    rows = pl.ds(pl.multiple_of(core * PIECE, PIECE), PIECE)
    residual = jnp.concatenate([hidden[rows, :], other[rows, :]], axis=0).astype(f32)
    sides = []
    for sequence in (core, 1 - core):
        heads = [attended[sequence * HEADS + head] for head in range(HEADS)]
        sides.append(jnp.concatenate(heads, axis=1))
    mixed = jnp.concatenate(sides, axis=0)
    first = residual + jnp.dot(mixed, w_output[...], preferred_element_type=f32)
    inner = layer_norm(first).astype(bf16)
    second = first
    for part in range(FF_PARTS):
        cut = slice(part * FF_PART, (part + 1) * FF_PART)
        expanded = jnp.dot(inner, w_up[:, cut], preferred_element_type=f32)
        expanded = jax.nn.gelu(expanded).astype(bf16)
        second = second + jnp.dot(expanded, w_down[cut, :], preferred_element_type=f32)
    features = layer_norm(second).astype(bf16)
    shift, log_scale = (
        lax.dot_general(
            weight[...], features, (((1,), (1,)), ((), ())), preferred_element_type=f32
        )
        for weight in (w_shift, w_scale)
    )
    determinant = -jnp.sum(log_scale, axis=0, keepdims=True)
    high = determinant.astype(bf16)
    low = (determinant - high.astype(f32)).astype(bf16)
    row = lax.broadcasted_iota(jnp.int32, (SENT - CHANNELS, TOKENS), 0)
    tail = jnp.where(row == 0, high.astype(f32), jnp.where(row == 1, low.astype(f32), 0.0))
    flows = []
    for source in (flow, other_flow):
        flows.append(jnp.where(core == 0, source[:, :PIECE].astype(f32), source[:, PIECE:].astype(f32)))
    moved = (jnp.concatenate(flows, axis=1) - shift) * jnp.exp(-log_scale)
    sent = jnp.concatenate([moved, tail], axis=0).astype(bf16)
    sent_own[...] = sent[:, :PIECE]
    sent_other[...] = sent[:, PIECE:]


def join_kernel(place, mine, theirs, latent, log_det):
    core = place[0]
    row = lax.broadcasted_iota(jnp.int32, (PIECE, TOKENS), 0)
    column = lax.broadcasted_iota(jnp.int32, (PIECE, TOKENS), 1)
    total = None
    for source, half in ((mine, core), (theirs, 1 - core)):
        chosen = (column == TOKENS - 1 - half * PIECE - row).astype(f32).astype(bf16)
        term = jnp.dot(source[...], chosen, preferred_element_type=f32)
        total = term if total is None else total + term
    latent[...] = total[:CHANNELS]
    log_det[...] = total[CHANNELS : CHANNELS + 1] + total[CHANNELS + 1 : CHANNELS + 2]


def shift_by(count, step):
    return [(index, (index + step) % count) for index in range(count)]


def on_device(
    hidden, flow_input, w_query, w_key, w_value, w_output, w_up, w_down, w_shift, w_scale
):
    core = lax.axis_index("core")
    z = lax.axis_index("z")
    query_z = Z - 1 - z
    up_steps = [(z - step) % Z - query_z for step in range(5)]
    down_steps = [(z + step) % Z - query_z for step in range(4)]
    place = jnp.stack([core, *up_steps, *down_steps]).astype(jnp.int32)
    other_core = shift_by(2, 1)
    other = lax.ppermute(hidden, "core", other_core)
    count = XL * Y * Z
    mirrored = [(index, count - 1 - index) for index in range(count)]
    far_hidden = lax.ppermute(hidden, ("xl", "y", "z"), mirrored)
    far_flow = lax.ppermute(flow_input, ("xl", "y", "z"), mirrored)
    other_far_hidden = lax.ppermute(far_hidden, "core", other_core)
    other_far_flow = lax.ppermute(far_flow, "core", other_core)

    square = pltpu.VMEM((WIDTH, INNER), bf16)
    own, *weights = pl.pallas_call(
        load_kernel,
        out_shape=[pltpu.VMEM((PIECE, WIDTH), bf16), square, square, square],
        in_specs=[smem()] + [hbm()] * 4,
        out_specs=[vmem()] * 4,
        scratch_shapes=[pltpu.SemaphoreType.DMA((12,)), pltpu.SemaphoreType.DMA],
        compiler_params=params(8),
        cost_estimate=pl.CostEstimate(flops=0, bytes_accessed=6_600_000, transcendentals=0),
    )(place, *(in_hbm(array) for array in (hidden, w_query, w_key, w_value)))
    slots = pl.pallas_call(
        qkv_kernel,
        out_shape=jax.ShapeDtypeStruct((PLANES, PIECE, 3 * HEAD), bf16),
        in_specs=[smem()] + [vmem()] * 5,
        out_specs=vmem(),
        scratch_shapes=[pltpu.VMEM((TOKENS, WIDTH), bf16)],
        compiler_params=params(8),
    )(place, own, other, *weights)
    slots = lax.all_to_all(slots, ("xl", "y"), 0, 0, tiled=True)
    chunk, queries = pl.pallas_call(
        pack_kernel,
        out_shape=[
            jax.ShapeDtypeStruct((2 * ROWS, HEAD), bf16),
            jax.ShapeDtypeStruct((PLANES, PIECE, HEAD), bf16),
        ],
        in_specs=[vmem()],
        out_specs=[vmem()] * 2,
        compiler_params=params(8),
    )(slots)
    queries = lax.ppermute(queries, "z", [(index, Z - 1 - index) for index in range(Z)])
    other_queries = lax.ppermute(queries, "core", other_core)

    whole = (0, 1)
    up = down = chunk
    queries, *state = attend(place, (queries, other_queries), [chunk], [(whole, 0)], None, False)
    early = {2: (other_far_hidden, other_far_flow)}
    for step in range(1, 4):
        up = lax.ppermute(up, "z", shift_by(Z, 1))
        down = lax.ppermute(down, "z", shift_by(Z, -1))
        state = attend(
            place,
            (queries,),
            [up, down],
            [(whole, step), (whole, 5 + step)],
            state,
            False,
            early.get(step, ()),
        )
    far = [
        lax.ppermute(up[:ROWS], "z", shift_by(Z, 1)),
        lax.ppermute(down[ROWS:], "z", shift_by(Z, -1)),
    ]
    mine, others = attend(place, (queries,), far, [((0,), 4), ((1,), 4)], state, True)
    theirs = lax.ppermute(others, "core", other_core)
    attended = pl.pallas_call(
        merge_kernel,
        out_shape=jax.ShapeDtypeStruct((PLANES, PIECE, HEAD), bf16),
        in_specs=[vmem()] * 2,
        out_specs=vmem(),
        compiler_params=params(8),
    )(mine, theirs)
    attended = lax.all_to_all(attended, ("xl", "y"), 0, 0, tiled=True)

    sent = jax.ShapeDtypeStruct((SENT, PIECE), bf16)
    sent_own, sent_other = pl.pallas_call(
        dense_kernel,
        out_shape=[sent, sent],
        in_specs=[smem()] + [vmem()] * 10,
        out_specs=[vmem()] * 2,
        compiler_params=params(16),
    )(
        place,
        attended,
        far_hidden,
        other_far_hidden,
        far_flow,
        other_far_flow,
        w_output,
        w_up,
        w_down,
        w_shift,
        w_scale,
    )
    received = lax.ppermute(sent_other, "core", other_core)
    latent, log_det = pl.pallas_call(
        join_kernel,
        out_shape=[
            jax.ShapeDtypeStruct((CHANNELS, TOKENS), f32),
            jax.ShapeDtypeStruct((1, TOKENS), f32),
        ],
        in_specs=[smem()] + [vmem()] * 2,
        out_specs=[vmem()] * 2,
        compiler_params=params(8),
    )(place, sent_own, received)
    return (latent, log_det.reshape(TOKENS))


def solution(mesh):
    parts = Mesh(mesh.devices.reshape(2, 2, XL, Y, Z), ("xh", "core", "xl", "y", "z"))
    everywhere = ("xh", "core", "xl", "y", "z")
    in_specs = (P(everywhere, None), P(None, everywhere)) + (P(),) * 8
    out_specs = (P(None, everywhere), P(everywhere))
    return jax.shard_map(
        on_device, mesh=parts, in_specs=in_specs, out_specs=out_specs, check_vma=False
    )
```

```python
import functools

import jax
import jax.numpy as jnp
from jax import lax
from jax.experimental import pallas as pl
from jax.experimental.pallas import tpu as pltpu
from jax.sharding import Mesh, PartitionSpec as P

HEADS = 4
HEAD = 128
WIDTH = 1024
INNER = HEADS * HEAD
FF = 2048
CHANNELS = 64
epsilon = 1e-05
masked_score = -2e30
lowest = -1e30
POWER = HEAD**-0.5 * 1.4426950408889634
bf16 = jnp.bfloat16
f32 = jnp.float32

XL, Y, Z = 2, 4, 8
PLANES = XL * Y
TOKENS = 192
PIECE = TOKENS // 2
ROWS = PLANES * PIECE
TILE = 2 * TOKENS
TILES = 2 * ROWS // TILE
HALF = ROWS // 2
BLOCKS = HALF // HEAD
FIRST_COST, COST = 4, 32
TALL = HEAD + 16
SENT = CHANNELS + 16


def layer_norm(values):
    mean = jnp.mean(values, axis=-1, keepdims=True)
    centred = values - mean
    spread = jnp.mean(centred * centred, axis=-1, keepdims=True)
    return centred * lax.rsqrt(spread + epsilon)


def vmem():
    return pl.BlockSpec(memory_space=pltpu.VMEM)


def smem():
    return pl.BlockSpec(memory_space=pltpu.SMEM)


def params(mebibytes):
    return pltpu.CompilerParams(vmem_limit_bytes=mebibytes << 20)


def in_hbm(array):
    return pltpu.with_memory_space_constraint(array, pltpu.HBM)


def hbm():
    return pl.BlockSpec(memory_space=pltpu.HBM)


def start_loads(sources, targets, sems):
    copies = []
    for source, target in zip(sources, targets):
        pieces = 4 if source.shape[0] >= 512 else 1
        size = source.shape[0] // pieces
        for piece in range(pieces):
            cut = pl.ds(piece * size, size)
            copies.append(
                pltpu.make_async_copy(source.at[cut], target.at[cut], sems.at[len(copies)])
            )
    for copy in copies:
        copy.start()
    return copies


def load_kernel(place, hidden, w_query, w_key, w_value, own, query, key, value, sems, own_sem):
    rows = pl.ds(pl.multiple_of(place[0] * PIECE, PIECE), PIECE)
    copy = pltpu.make_async_copy(hidden.at[rows], own, own_sem)
    copy.start()
    copies = start_loads((w_key, w_value, w_query), (key, value, query), sems)
    copy.wait()
    for copy in copies:
        copy.wait()


def qkv_kernel(place, own, other, w_query, w_key, w_value, slots, normed):
    core = place[0]
    normed[:PIECE, :] = layer_norm(own[...].astype(f32)).astype(bf16)
    rows = pl.ds(pl.multiple_of(core * PIECE, PIECE), PIECE)
    normed[PIECE:, :] = layer_norm(other[rows, :].astype(f32)).astype(bf16)
    for column, weight in enumerate((w_query, w_key, w_value)):
        made = jnp.dot(normed[...], weight[...], preferred_element_type=f32).astype(bf16)
        for part in range(2):
            sequence = core if part == 0 else 1 - core
            for head in range(HEADS):
                slots[sequence * HEADS + head, :, column * HEAD : (column + 1) * HEAD] = made[
                    part * PIECE : (part + 1) * PIECE, head * HEAD : (head + 1) * HEAD
                ]


def pack_kernel(slots, chunk, queries):
    for part in range(2):
        first = part * (PLANES // 2)
        base = part * ROWS
        values = []
        for plane in range(PLANES // 2):
            start = base + plane * PIECE
            chunk[start : start + PIECE, :] = slots[first + plane, :, HEAD : 2 * HEAD]
            values.append(slots[first + plane, :, 2 * HEAD :])
        values = jnp.concatenate(values, axis=0)
        for block in range(BLOCKS):
            square = values[block * HEAD : (block + 1) * HEAD, :].astype(f32)
            start = base + HALF + block * HEAD
            chunk[start : start + HEAD, :] = square.T.astype(bf16)
    queries[...] = slots[:, :, :HEAD]


def attend_kernel(chunks, first, last, after, *refs):
    refs = list(refs)
    place = refs.pop(0)
    if first:
        own, other = refs.pop(0), refs.pop(0)
    else:
        queries = refs.pop(0)
    segments = []
    for halves, source in chunks:
        chunk = refs.pop(0)
        for index, part in enumerate(halves):
            segments.append((chunk, index * ROWS, part, source))
    if not first:
        top_in, numer_in = refs.pop(0), refs.pop(0)
    refs = refs[after:]
    if first:
        queries = refs.pop(0)
        for tile in range(TILES):
            planes = (2 * tile, 2 * tile + 1)
            rows = [own[plane] for plane in planes] + [other[plane] for plane in planes]
            turned = jnp.concatenate(rows, axis=0).astype(f32).T
            queries[:, tile * TILE : (tile + 1) * TILE] = turned.astype(bf16)
    core = place[0]
    column = lax.broadcasted_iota(jnp.int32, (1, TILE), 1)
    column_half = jnp.where(column < TOKENS, core, 1 - core)
    column_plane = (column % TOKENS) // PIECE
    column_place = column_plane * (Z * TOKENS) + column_half * PIECE + column % PIECE
    key = lax.broadcasted_iota(jnp.int32, (HALF, 1), 0)
    key_place = (key // PIECE) * (Z * TOKENS) + key % PIECE + core * PIECE
    ones = jnp.ones((TALL - HEAD, HALF), bf16)
    values = []
    for chunk, base, _, _ in segments:
        starts = [base + HALF + index * HEAD for index in range(BLOCKS)]
        blocks = [chunk[start : start + HEAD, :] for start in starts]
        values.append(jnp.concatenate([jnp.concatenate(blocks, axis=1), ones], axis=0))

    def score(tile):
        columns = slice(tile * TILE, (tile + 1) * TILE)
        found = []
        for (chunk, base, part, source), value in zip(segments, values):
            groups = min(2, tile + 1 - 2 * part)
            if groups <= 0:
                continue
            count = groups * TOKENS
            product = jnp.dot(
                chunk[base : base + count, :], queries[:, columns], preferred_element_type=f32
            )
            if 2 * part + groups - 1 == tile:
                shift = place[1 + source] * TOKENS
                offset = 2 * (tile - 2 * part) * (Z * TOKENS)
                allowed = key_place[:count] + shift <= column_place + offset
                product = jnp.where(allowed, product, masked_score)
            found.append((value[:, :count], product))
        return found

    def finish(tile, found):
        columns = slice(tile * TILE, (tile + 1) * TILE)
        top = jnp.full((1, TILE), lowest, f32) if first else top_in[:1, columns]
        new_top = top
        for _, product in found:
            new_top = jnp.maximum(new_top, jnp.max(product, axis=0, keepdims=True))
        if first:
            sums = jnp.zeros((TALL, TILE), f32)
        else:
            sums = numer_in[:, columns] * jnp.exp2((top - new_top) * POWER)
        for value, product in found:
            weights = jnp.exp2((product - new_top) * POWER).astype(bf16)
            sums = sums + jnp.dot(value, weights, preferred_element_type=f32)
        if not last:
            top_out, numer_out = refs
            top_out[:, columns] = jnp.broadcast_to(new_top, (8, TILE))
            numer_out[:, columns] = sums
            return
        total = sums[HEAD : HEAD + 1, :]
        some = total > 0
        total = jnp.where(some, total, 1.0)
        mixed = (sums[:HEAD, :] / total).T
        level = jnp.where(some, new_top * POWER + jnp.log2(total), lowest)
        level = jnp.broadcast_to(level, (HEAD, TILE)).T
        high = level.astype(bf16)
        rest = level - high.astype(f32)
        middle = rest.astype(bf16)
        low = (rest - middle.astype(f32)).astype(bf16)
        lane = lax.broadcasted_iota(jnp.int32, (TILE, HEAD), 1)
        level = jnp.where(lane == 0, high, jnp.where(lane == 1, middle, low))
        for side in range(2):
            for plane in range(2):
                start = side * TOKENS + plane * PIECE
                refs[side][2 * tile + plane, :, :HEAD] = mixed[start : start + PIECE].astype(bf16)
                refs[side][2 * tile + plane, :, HEAD:] = level[start : start + PIECE]

    found = score(0)
    for tile in range(TILES):
        following = score(tile + 1) if tile + 1 < TILES else None
        finish(tile, found)
        found = following


def attend(place, queries, segments, chunks, state, last, after=()):
    first = state is None
    count = sum(len(halves) for halves, _ in chunks)
    stats = [jax.ShapeDtypeStruct((8, 2 * ROWS), f32), jax.ShapeDtypeStruct((TALL, 2 * ROWS), f32)]
    if last:
        shapes = [jax.ShapeDtypeStruct((PLANES, PIECE, 2 * HEAD), bf16)] * 2
    elif first:
        shapes = [jax.ShapeDtypeStruct((HEAD, 2 * ROWS), bf16), *stats]
    else:
        shapes = stats
    operands = [place, *queries, *segments, *(state or ()), *after]
    return pl.pallas_call(
        functools.partial(attend_kernel, chunks, first, last, len(after)),
        out_shape=shapes,
        in_specs=[smem()] + [vmem()] * (len(operands) - 1),
        out_specs=[vmem()] * len(shapes),
        compiler_params=params(16),
        cost_estimate=pl.CostEstimate(
            flops=(FIRST_COST if first else COST) * ROWS * HALF * HEAD * count,
            bytes_accessed=3_000_000,
            transcendentals=ROWS * HALF * count,
        ),
    )(*operands)


def merge_kernel(mine, theirs, out):
    row = lax.broadcasted_iota(jnp.int32, (HEAD, HEAD), 0)
    spread = (row < 3).astype(f32).astype(bf16)

    def level(block):
        stats = block[:, :, HEAD:].reshape(ROWS, HEAD)
        return jnp.dot(stats, spread, preferred_element_type=f32)

    first, second = level(mine), level(theirs)
    top = jnp.maximum(first, second)
    first, second = jnp.exp2(first - top), jnp.exp2(second - top)
    both = first * mine[:, :, :HEAD].reshape(ROWS, HEAD).astype(f32)
    both = both + second * theirs[:, :, :HEAD].reshape(ROWS, HEAD).astype(f32)
    both = (both / (first + second)).astype(bf16).reshape(PLANES, PIECE, HEAD)
    out[...] = both


FF_PARTS = 2
FF_PART = FF // FF_PARTS


def dense_kernel(
    place,
    attended,
    own,
    other,
    flow,
    other_flow,
    w_output,
    w_up,
    w_down,
    w_shift,
    w_scale,
    sent_own,
    sent_other,
):
    core = place[0]
    rows = pl.ds(pl.multiple_of(core * PIECE, PIECE), PIECE)
    residual = jnp.concatenate([own[...], other[rows, :]], axis=0).astype(f32)
    sides = []
    for sequence in (core, 1 - core):
        heads = [attended[sequence * HEADS + head] for head in range(HEADS)]
        sides.append(jnp.concatenate(heads, axis=1))
    mixed = jnp.concatenate(sides, axis=0)
    first = residual + jnp.dot(mixed, w_output[...], preferred_element_type=f32)
    inner = layer_norm(first).astype(bf16)
    second = first
    for part in range(FF_PARTS):
        cut = slice(part * FF_PART, (part + 1) * FF_PART)
        expanded = jnp.dot(inner, w_up[:, cut], preferred_element_type=f32)
        expanded = jax.nn.gelu(expanded).astype(bf16)
        second = second + jnp.dot(expanded, w_down[cut, :], preferred_element_type=f32)
    features = layer_norm(second).astype(bf16)
    shift, log_scale = (
        lax.dot_general(
            weight[...], features, (((1,), (1,)), ((), ())), preferred_element_type=f32
        )
        for weight in (w_shift, w_scale)
    )
    determinant = -jnp.sum(log_scale, axis=0, keepdims=True)
    high = determinant.astype(bf16)
    low = (determinant - high.astype(f32)).astype(bf16)
    row = lax.broadcasted_iota(jnp.int32, (SENT - CHANNELS, TOKENS), 0)
    tail = jnp.where(row == 0, high.astype(f32), jnp.where(row == 1, low.astype(f32), 0.0))
    flows = []
    for source in (flow, other_flow):
        flows.append(jnp.where(core == 0, source[:, :PIECE].astype(f32), source[:, PIECE:].astype(f32)))
    moved = (jnp.concatenate(flows, axis=1) - shift) * jnp.exp(-log_scale)
    sent = jnp.concatenate([moved, tail], axis=0).astype(bf16)
    sent_own[...] = sent[:, :PIECE]
    sent_other[...] = sent[:, PIECE:]


def join_kernel(place, mine, theirs, out):
    core = place[0]
    row = lax.broadcasted_iota(jnp.int32, (PIECE, TOKENS), 0)
    column = lax.broadcasted_iota(jnp.int32, (PIECE, TOKENS), 1)
    total = None
    for source, half in ((mine, core), (theirs, 1 - core)):
        chosen = (column == TOKENS - 1 - half * PIECE - row).astype(f32).astype(bf16)
        term = jnp.dot(source[...], chosen, preferred_element_type=f32)
        total = term if total is None else total + term
    out[...] = total.astype(bf16)


def shift_by(count, step):
    return [(index, (index + step) % count) for index in range(count)]


def on_device(
    hidden, flow_input, w_query, w_key, w_value, w_output, w_up, w_down, w_shift, w_scale
):
    core = lax.axis_index("core")
    z = lax.axis_index("z")
    up_steps = [(z - step) % Z - z for step in range(5)]
    down_steps = [(z + step) % Z - z for step in range(4)]
    place = jnp.stack([core, *up_steps, *down_steps]).astype(jnp.int32)
    other_core = shift_by(2, 1)
    other = lax.ppermute(hidden, "core", other_core)
    other_flow = lax.ppermute(flow_input, "core", other_core)

    square = pltpu.VMEM((WIDTH, INNER), bf16)
    own, *weights = pl.pallas_call(
        load_kernel,
        out_shape=[pltpu.VMEM((PIECE, WIDTH), bf16), square, square, square],
        in_specs=[smem()] + [hbm()] * 4,
        out_specs=[vmem()] * 4,
        scratch_shapes=[pltpu.SemaphoreType.DMA((12,)), pltpu.SemaphoreType.DMA],
        compiler_params=params(8),
        cost_estimate=pl.CostEstimate(flops=0, bytes_accessed=6_600_000, transcendentals=0),
    )(place, *(in_hbm(array) for array in (hidden, w_query, w_key, w_value)))
    slots = pl.pallas_call(
        qkv_kernel,
        out_shape=jax.ShapeDtypeStruct((PLANES, PIECE, 3 * HEAD), bf16),
        in_specs=[smem()] + [vmem()] * 5,
        out_specs=vmem(),
        scratch_shapes=[pltpu.VMEM((TOKENS, WIDTH), bf16)],
        compiler_params=params(8),
    )(place, own, other, *weights)
    slots = lax.all_to_all(slots, ("xl", "y"), 0, 0, tiled=True)
    chunk, queries = pl.pallas_call(
        pack_kernel,
        out_shape=[
            jax.ShapeDtypeStruct((2 * ROWS, HEAD), bf16),
            jax.ShapeDtypeStruct((PLANES, PIECE, HEAD), bf16),
        ],
        in_specs=[vmem()],
        out_specs=[vmem()] * 2,
        compiler_params=params(8),
    )(slots)
    other_queries = lax.ppermute(queries, "core", other_core)

    whole = (0, 1)
    up = down = chunk
    queries, *state = attend(place, (queries, other_queries), [chunk], [(whole, 0)], None, False)
    early = {1: (other_flow,)}
    for step in range(1, 4):
        up = lax.ppermute(up, "z", shift_by(Z, 1))
        down = lax.ppermute(down, "z", shift_by(Z, -1))
        state = attend(
            place,
            (queries,),
            [up, down],
            [(whole, step), (whole, 5 + step)],
            state,
            False,
            early.get(step, ()),
        )
    far = [
        lax.ppermute(up[:ROWS], "z", shift_by(Z, 1)),
        lax.ppermute(down[ROWS:], "z", shift_by(Z, -1)),
    ]
    mine, others = attend(place, (queries,), far, [((0,), 4), ((1,), 4)], state, True)
    theirs = lax.ppermute(others, "core", other_core)
    attended = pl.pallas_call(
        merge_kernel,
        out_shape=jax.ShapeDtypeStruct((PLANES, PIECE, HEAD), bf16),
        in_specs=[vmem()] * 2,
        out_specs=vmem(),
        compiler_params=params(8),
    )(mine, theirs)
    attended = lax.all_to_all(attended, ("xl", "y"), 0, 0, tiled=True)

    sent = jax.ShapeDtypeStruct((SENT, PIECE), bf16)
    sent_own, sent_other = pl.pallas_call(
        dense_kernel,
        out_shape=[sent, sent],
        in_specs=[smem()] + [vmem()] * 10,
        out_specs=[vmem()] * 2,
        compiler_params=params(16),
    )(
        place,
        attended,
        own,
        other,
        flow_input,
        other_flow,
        w_output,
        w_up,
        w_down,
        w_shift,
        w_scale,
    )
    received = lax.ppermute(sent_other, "core", other_core)
    block = pl.pallas_call(
        join_kernel,
        out_shape=jax.ShapeDtypeStruct((SENT, TOKENS), bf16),
        in_specs=[smem()] + [vmem()] * 2,
        out_specs=vmem(),
        compiler_params=params(8),
    )(place, sent_own, received)
    count = XL * Y * Z
    mirrored = [(index, count - 1 - index) for index in range(count)]
    arrived = lax.ppermute(block, ("xl", "y", "z"), mirrored).astype(f32)
    return (arrived[:CHANNELS], arrived[CHANNELS] + arrived[CHANNELS + 1])


def solution(mesh):
    parts = Mesh(mesh.devices.reshape(2, 2, XL, Y, Z), ("xh", "core", "xl", "y", "z"))
    everywhere = ("xh", "core", "xl", "y", "z")
    in_specs = (P(everywhere, None), P(None, everywhere)) + (P(),) * 8
    out_specs = (P(None, everywhere), P(everywhere))
    return jax.shard_map(
        on_device, mesh=parts, in_specs=in_specs, out_specs=out_specs, check_vma=False
    )
```

```python
import functools

import jax
import jax.numpy as jnp
from jax import lax
from jax.experimental import pallas as pl
from jax.experimental.pallas import tpu as pltpu
from jax.sharding import Mesh, PartitionSpec as P

HEADS = 4
HEAD = 128
WIDTH = 1024
INNER = HEADS * HEAD
FF = 2048
CHANNELS = 64
epsilon = 1e-05
masked_score = -2e30
lowest = -1e30
POWER = HEAD**-0.5 * 1.4426950408889634
bf16 = jnp.bfloat16
f32 = jnp.float32

XL, Y, Z = 2, 4, 8
PLANES = XL * Y
TOKENS = 192
PIECE = TOKENS // 2
ROWS = PLANES * PIECE
TILE = 2 * TOKENS
TILES = 2 * ROWS // TILE
HALF = ROWS // 2
BLOCKS = HALF // HEAD
FIRST_COST, COST = 4, 32
AFTER = 2
TALL = HEAD + 16
SENT = CHANNELS + 16


def layer_norm(values):
    mean = jnp.mean(values, axis=-1, keepdims=True)
    centred = values - mean
    spread = jnp.mean(centred * centred, axis=-1, keepdims=True)
    return centred * lax.rsqrt(spread + epsilon)


def vmem():
    return pl.BlockSpec(memory_space=pltpu.VMEM)


def smem():
    return pl.BlockSpec(memory_space=pltpu.SMEM)


def params(mebibytes):
    return pltpu.CompilerParams(vmem_limit_bytes=mebibytes << 20)


def in_hbm(array):
    return pltpu.with_memory_space_constraint(array, pltpu.HBM)


def hbm():
    return pl.BlockSpec(memory_space=pltpu.HBM)


def start_loads(sources, targets, sems):
    copies = []
    for source, target in zip(sources, targets):
        pieces = 4 if source.shape[0] >= 512 else 1
        size = source.shape[0] // pieces
        for piece in range(pieces):
            cut = pl.ds(piece * size, size)
            copies.append(
                pltpu.make_async_copy(source.at[cut], target.at[cut], sems.at[len(copies)])
            )
    for copy in copies:
        copy.start()
    return copies


def load_kernel(place, hidden, w_query, w_key, w_value, own, query, key, value, sems, own_sem):
    rows = pl.ds(pl.multiple_of(place[0] * PIECE, PIECE), PIECE)
    copy = pltpu.make_async_copy(hidden.at[rows], own, own_sem)
    copy.start()
    copies = start_loads((w_key, w_value, w_query), (key, value, query), sems)
    copy.wait()
    for copy in copies:
        copy.wait()


def qkv_kernel(place, own, other, w_query, w_key, w_value, slots, normed):
    core = place[0]
    normed[:PIECE, :] = layer_norm(own[...].astype(f32)).astype(bf16)
    rows = pl.ds(pl.multiple_of(core * PIECE, PIECE), PIECE)
    normed[PIECE:, :] = layer_norm(other[rows, :].astype(f32)).astype(bf16)
    for column, weight in enumerate((w_query, w_key, w_value)):
        made = jnp.dot(normed[...], weight[...], preferred_element_type=f32).astype(bf16)
        for part in range(2):
            sequence = core if part == 0 else 1 - core
            for head in range(HEADS):
                slots[sequence * HEADS + head, :, column * HEAD : (column + 1) * HEAD] = made[
                    part * PIECE : (part + 1) * PIECE, head * HEAD : (head + 1) * HEAD
                ]


def both_kernel(place, own, other, flow, other_flow, token, both):
    del token
    core = place[0]
    rows = pl.ds(pl.multiple_of(core * PIECE, PIECE), PIECE)
    both[:PIECE, :] = own[...]
    both[PIECE:TOKENS, :] = other[rows, :]
    both[TOKENS:, :] = jnp.zeros((CHANNELS, WIDTH), bf16)
    flows = []
    for source in (flow, other_flow):
        flows.append(jnp.where(core == 0, source[:, :PIECE].astype(f32), source[:, PIECE:].astype(f32)))
    both[TOKENS:, :TOKENS] = jnp.concatenate(flows, axis=1).astype(bf16)


def pack_kernel(slots, chunk, queries):
    for part in range(2):
        first = part * (PLANES // 2)
        base = part * ROWS
        values = []
        for plane in range(PLANES // 2):
            start = base + plane * PIECE
            chunk[start : start + PIECE, :] = slots[first + plane, :, HEAD : 2 * HEAD]
            values.append(slots[first + plane, :, 2 * HEAD :])
        values = jnp.concatenate(values, axis=0)
        for block in range(BLOCKS):
            square = values[block * HEAD : (block + 1) * HEAD, :].astype(f32)
            start = base + HALF + block * HEAD
            chunk[start : start + HEAD, :] = square.T.astype(bf16)
    queries[...] = slots[:, :, :HEAD]


def attend_kernel(chunks, first, last, after, *refs):
    refs = list(refs)
    place = refs.pop(0)
    if first:
        own, other = refs.pop(0), refs.pop(0)
    else:
        queries = refs.pop(0)
    segments = []
    for halves, source in chunks:
        chunk = refs.pop(0)
        for index, part in enumerate(halves):
            segments.append((chunk, index * ROWS, part, source))
    if not first:
        top_in, numer_in = refs.pop(0), refs.pop(0)
    refs = refs[after:]
    if first:
        queries = refs.pop(0)
        for tile in range(TILES):
            planes = (2 * tile, 2 * tile + 1)
            rows = [own[plane] for plane in planes] + [other[plane] for plane in planes]
            turned = jnp.concatenate(rows, axis=0).astype(f32).T
            queries[:, tile * TILE : (tile + 1) * TILE] = turned.astype(bf16)
    core = place[0]
    column = lax.broadcasted_iota(jnp.int32, (1, TILE), 1)
    column_half = jnp.where(column < TOKENS, core, 1 - core)
    column_plane = (column % TOKENS) // PIECE
    column_place = column_plane * (Z * TOKENS) + column_half * PIECE + column % PIECE
    key = lax.broadcasted_iota(jnp.int32, (HALF, 1), 0)
    key_place = (key // PIECE) * (Z * TOKENS) + key % PIECE + core * PIECE
    ones = jnp.ones((TALL - HEAD, HALF), bf16)
    values = []
    for chunk, base, _, _ in segments:
        starts = [base + HALF + index * HEAD for index in range(BLOCKS)]
        blocks = [chunk[start : start + HEAD, :] for start in starts]
        values.append(jnp.concatenate([jnp.concatenate(blocks, axis=1), ones], axis=0))

    def score(tile):
        columns = slice(tile * TILE, (tile + 1) * TILE)
        found = []
        for (chunk, base, part, source), value in zip(segments, values):
            groups = min(2, tile + 1 - 2 * part)
            if groups <= 0:
                continue
            count = groups * TOKENS
            product = jnp.dot(
                chunk[base : base + count, :], queries[:, columns], preferred_element_type=f32
            )
            if 2 * part + groups - 1 == tile:
                shift = place[1 + source] * TOKENS
                offset = 2 * (tile - 2 * part) * (Z * TOKENS)
                allowed = key_place[:count] + shift <= column_place + offset
                product = jnp.where(allowed, product, masked_score)
            found.append((value[:, :count], product))
        return found

    def finish(tile, found):
        columns = slice(tile * TILE, (tile + 1) * TILE)
        top = jnp.full((1, TILE), lowest, f32) if first else top_in[:1, columns]
        new_top = top
        for _, product in found:
            new_top = jnp.maximum(new_top, jnp.max(product, axis=0, keepdims=True))
        if first:
            sums = jnp.zeros((TALL, TILE), f32)
        else:
            sums = numer_in[:, columns] * jnp.exp2((top - new_top) * POWER)
        for value, product in found:
            weights = jnp.exp2((product - new_top) * POWER).astype(bf16)
            sums = sums + jnp.dot(value, weights, preferred_element_type=f32)
        if not last:
            top_out, numer_out = refs
            top_out[:, columns] = jnp.broadcast_to(new_top, (8, TILE))
            numer_out[:, columns] = sums
            return
        total = sums[HEAD : HEAD + 1, :]
        some = total > 0
        total = jnp.where(some, total, 1.0)
        mixed = (sums[:HEAD, :] / total).T
        level = jnp.where(some, new_top * POWER + jnp.log2(total), lowest)
        level = jnp.broadcast_to(level, (HEAD, TILE)).T
        high = level.astype(bf16)
        rest = level - high.astype(f32)
        middle = rest.astype(bf16)
        low = (rest - middle.astype(f32)).astype(bf16)
        lane = lax.broadcasted_iota(jnp.int32, (TILE, HEAD), 1)
        level = jnp.where(lane == 0, high, jnp.where(lane == 1, middle, low))
        for side in range(2):
            for plane in range(2):
                start = side * TOKENS + plane * PIECE
                refs[side][2 * tile + plane, :, :HEAD] = mixed[start : start + PIECE].astype(bf16)
                refs[side][2 * tile + plane, :, HEAD:] = level[start : start + PIECE]

    found = score(0)
    for tile in range(TILES):
        following = score(tile + 1) if tile + 1 < TILES else None
        finish(tile, found)
        found = following


def attend(place, queries, segments, chunks, state, last, after=()):
    first = state is None
    count = sum(len(halves) for halves, _ in chunks)
    stats = [jax.ShapeDtypeStruct((8, 2 * ROWS), f32), jax.ShapeDtypeStruct((TALL, 2 * ROWS), f32)]
    if last:
        shapes = [jax.ShapeDtypeStruct((PLANES, PIECE, 2 * HEAD), bf16)] * 2
    elif first:
        shapes = [jax.ShapeDtypeStruct((HEAD, 2 * ROWS), bf16), *stats]
    else:
        shapes = stats
    operands = [place, *queries, *segments, *(state or ()), *after]
    return pl.pallas_call(
        functools.partial(attend_kernel, chunks, first, last, len(after)),
        out_shape=shapes,
        in_specs=[smem()] + [vmem()] * (len(operands) - 1),
        out_specs=[vmem()] * len(shapes),
        compiler_params=params(16),
        cost_estimate=pl.CostEstimate(
            flops=(FIRST_COST if first else COST) * ROWS * HALF * HEAD * count,
            bytes_accessed=3_000_000,
            transcendentals=ROWS * HALF * count,
        ),
    )(*operands)


def merge_kernel(mine, theirs, out):
    row = lax.broadcasted_iota(jnp.int32, (HEAD, HEAD), 0)
    spread = (row < 3).astype(f32).astype(bf16)

    def level(block):
        stats = block[:, :, HEAD:].reshape(ROWS, HEAD)
        return jnp.dot(stats, spread, preferred_element_type=f32)

    first, second = level(mine), level(theirs)
    top = jnp.maximum(first, second)
    first, second = jnp.exp2(first - top), jnp.exp2(second - top)
    both = first * mine[:, :, :HEAD].reshape(ROWS, HEAD).astype(f32)
    both = both + second * theirs[:, :, :HEAD].reshape(ROWS, HEAD).astype(f32)
    both = (both / (first + second)).astype(bf16).reshape(PLANES, PIECE, HEAD)
    for plane in range(PLANES):
        out[PLANES - 1 - plane] = both[plane]


FF_PARTS = 2
FF_PART = FF // FF_PARTS


def dense_kernel(
    place,
    attended,
    both,
    w_output,
    w_up,
    w_down,
    w_shift,
    w_scale,
    sent_own,
    sent_other,
):
    core = place[0]
    residual = both[:TOKENS, :].astype(f32)
    sides = []
    for sequence in (core, 1 - core):
        heads = [attended[sequence * HEADS + head] for head in range(HEADS)]
        sides.append(jnp.concatenate(heads, axis=1))
    mixed = jnp.concatenate(sides, axis=0)
    first = residual + jnp.dot(mixed, w_output[...], preferred_element_type=f32)
    inner = layer_norm(first).astype(bf16)
    second = first
    for part in range(FF_PARTS):
        cut = slice(part * FF_PART, (part + 1) * FF_PART)
        expanded = jnp.dot(inner, w_up[:, cut], preferred_element_type=f32)
        expanded = jax.nn.gelu(expanded).astype(bf16)
        second = second + jnp.dot(expanded, w_down[cut, :], preferred_element_type=f32)
    features = layer_norm(second).astype(bf16)
    shift, log_scale = (
        lax.dot_general(
            weight[...], features, (((1,), (1,)), ((), ())), preferred_element_type=f32
        )
        for weight in (w_shift, w_scale)
    )
    determinant = -jnp.sum(log_scale, axis=0, keepdims=True)
    high = determinant.astype(bf16)
    low = (determinant - high.astype(f32)).astype(bf16)
    row = lax.broadcasted_iota(jnp.int32, (SENT - CHANNELS, TOKENS), 0)
    tail = jnp.where(row == 0, high.astype(f32), jnp.where(row == 1, low.astype(f32), 0.0))
    flow = both[TOKENS:, :TOKENS].astype(f32)
    moved = (flow - shift) * jnp.exp(-log_scale)
    sent = jnp.concatenate([moved, tail], axis=0).astype(bf16)
    sent_own[...] = sent[:, :PIECE]
    sent_other[...] = sent[:, PIECE:]


def join_kernel(place, mine, theirs, out):
    core = place[0]
    row = lax.broadcasted_iota(jnp.int32, (PIECE, TOKENS), 0)
    column = lax.broadcasted_iota(jnp.int32, (PIECE, TOKENS), 1)
    total = None
    for source, half in ((mine, core), (theirs, 1 - core)):
        chosen = (column == TOKENS - 1 - half * PIECE - row).astype(f32).astype(bf16)
        term = jnp.dot(source[...], chosen, preferred_element_type=f32)
        total = term if total is None else total + term
    out[...] = total.astype(bf16)


def final_kernel(block, latent, log_det):
    latent[...] = block[:CHANNELS, :].astype(f32)
    det = block[CHANNELS:, :].astype(f32)
    log_det[...] = det[:1] + det[1:2]


def shift_by(count, step):
    return [(index, (index + step) % count) for index in range(count)]


def on_device(
    hidden, flow_input, w_query, w_key, w_value, w_output, w_up, w_down, w_shift, w_scale
):
    core = lax.axis_index("core")
    z = lax.axis_index("z")
    up_steps = [(z - step) % Z - z for step in range(5)]
    down_steps = [(z + step) % Z - z for step in range(4)]
    place = jnp.stack([core, *up_steps, *down_steps]).astype(jnp.int32)
    other_core = shift_by(2, 1)
    other = lax.ppermute(hidden, "core", other_core)
    other_flow = lax.ppermute(flow_input, "core", other_core)

    square = pltpu.VMEM((WIDTH, INNER), bf16)
    own, *weights = pl.pallas_call(
        load_kernel,
        out_shape=[pltpu.VMEM((PIECE, WIDTH), bf16), square, square, square],
        in_specs=[smem()] + [hbm()] * 4,
        out_specs=[vmem()] * 4,
        scratch_shapes=[pltpu.SemaphoreType.DMA((12,)), pltpu.SemaphoreType.DMA],
        compiler_params=params(8),
        cost_estimate=pl.CostEstimate(flops=0, bytes_accessed=6_600_000, transcendentals=0),
    )(place, *(in_hbm(array) for array in (hidden, w_query, w_key, w_value)))
    slots = pl.pallas_call(
        qkv_kernel,
        out_shape=jax.ShapeDtypeStruct((PLANES, PIECE, 3 * HEAD), bf16),
        in_specs=[smem()] + [vmem()] * 5,
        out_specs=vmem(),
        scratch_shapes=[pltpu.VMEM((TOKENS, WIDTH), bf16)],
        compiler_params=params(8),
    )(place, own, other, *weights)
    slots = lax.all_to_all(slots, ("xl", "y"), 0, 0, tiled=True)
    chunk, queries = pl.pallas_call(
        pack_kernel,
        out_shape=[
            jax.ShapeDtypeStruct((2 * ROWS, HEAD), bf16),
            jax.ShapeDtypeStruct((PLANES, PIECE, HEAD), bf16),
        ],
        in_specs=[vmem()],
        out_specs=[vmem()] * 2,
        compiler_params=params(8),
    )(slots)
    other_queries = lax.ppermute(queries, "core", other_core)

    whole = (0, 1)
    up = down = chunk
    queries, *state = attend(place, (queries, other_queries), [chunk], [(whole, 0)], None, False)
    both = pl.pallas_call(
        both_kernel,
        out_shape=jax.ShapeDtypeStruct((TOKENS + CHANNELS, WIDTH), bf16),
        in_specs=[smem()] + [vmem()] * 5,
        out_specs=vmem(),
        compiler_params=params(8),
    )(place, own, other, flow_input, other_flow, state[0])
    opposite = [(plane, PLANES - 1 - plane) for plane in range(PLANES)]
    both = lax.ppermute(both, ("xl", "y"), opposite)
    early = {AFTER: (both,)}
    for step in range(1, 4):
        up = lax.ppermute(up, "z", shift_by(Z, 1))
        down = lax.ppermute(down, "z", shift_by(Z, -1))
        state = attend(
            place,
            (queries,),
            [up, down],
            [(whole, step), (whole, 5 + step)],
            state,
            False,
            early.get(step, ()),
        )
    far = [
        lax.ppermute(up[:ROWS], "z", shift_by(Z, 1)),
        lax.ppermute(down[ROWS:], "z", shift_by(Z, -1)),
    ]
    mine, others = attend(place, (queries,), far, [((0,), 4), ((1,), 4)], state, True)
    theirs = lax.ppermute(others, "core", other_core)
    attended = pl.pallas_call(
        merge_kernel,
        out_shape=jax.ShapeDtypeStruct((PLANES, PIECE, HEAD), bf16),
        in_specs=[vmem()] * 2,
        out_specs=vmem(),
        compiler_params=params(8),
    )(mine, theirs)
    attended = lax.all_to_all(attended, ("xl", "y"), 0, 0, tiled=True)

    sent = jax.ShapeDtypeStruct((SENT, PIECE), bf16)
    sent_own, sent_other = pl.pallas_call(
        dense_kernel,
        out_shape=[sent, sent],
        in_specs=[smem()] + [vmem()] * 7,
        out_specs=[vmem()] * 2,
        compiler_params=params(16),
    )(
        place,
        attended,
        both,
        w_output,
        w_up,
        w_down,
        w_shift,
        w_scale,
    )
    received = lax.ppermute(sent_other, "core", other_core)
    block = pl.pallas_call(
        join_kernel,
        out_shape=jax.ShapeDtypeStruct((SENT, TOKENS), bf16),
        in_specs=[smem()] + [vmem()] * 2,
        out_specs=vmem(),
        compiler_params=params(8),
    )(place, sent_own, received)
    block = lax.ppermute(block, "z", [(index, Z - 1 - index) for index in range(Z)])
    latent, log_det = pl.pallas_call(
        final_kernel,
        out_shape=[
            jax.ShapeDtypeStruct((CHANNELS, TOKENS), f32),
            jax.ShapeDtypeStruct((1, TOKENS), f32),
        ],
        in_specs=[vmem()],
        out_specs=[vmem()] * 2,
        compiler_params=params(4),
    )(block)
    return (latent, log_det.reshape(TOKENS))


def solution(mesh):
    parts = Mesh(mesh.devices.reshape(2, 2, XL, Y, Z), ("xh", "core", "xl", "y", "z"))
    everywhere = ("xh", "core", "xl", "y", "z")
    in_specs = (P(everywhere, None), P(None, everywhere)) + (P(),) * 8
    out_specs = (P(None, everywhere), P(everywhere))
    return jax.shard_map(
        on_device, mesh=parts, in_specs=in_specs, out_specs=out_specs, check_vma=False
    )
```

```python
import functools

import jax
import jax.numpy as jnp
from jax import lax
from jax.experimental import pallas as pl
from jax.experimental.pallas import tpu as pltpu
from jax.sharding import Mesh, PartitionSpec as P

HEADS = 4
HEAD = 128
WIDTH = 1024
INNER = HEADS * HEAD
FF = 2048
CHANNELS = 64
epsilon = 1e-05
masked_score = -2e30
lowest = -1e30
POWER = HEAD**-0.5 * 1.4426950408889634
bf16 = jnp.bfloat16
f32 = jnp.float32

XL, Y, Z = 2, 4, 8
PLANES = XL * Y
TOKENS = 192
PIECE = TOKENS // 2
ROWS = PLANES * PIECE
TILE = 2 * TOKENS
TILES = 2 * ROWS // TILE
HALF = ROWS // 2
BLOCKS = HALF // HEAD
FIRST_COST, COST = 4, 32
AFTER = 2
TALL = HEAD + 16
SENT = CHANNELS + 16


def layer_norm(values):
    mean = jnp.mean(values, axis=-1, keepdims=True)
    centred = values - mean
    spread = jnp.mean(centred * centred, axis=-1, keepdims=True)
    return centred * lax.rsqrt(spread + epsilon)


def vmem():
    return pl.BlockSpec(memory_space=pltpu.VMEM)


def smem():
    return pl.BlockSpec(memory_space=pltpu.SMEM)


def params(mebibytes):
    return pltpu.CompilerParams(vmem_limit_bytes=mebibytes << 20)


def in_hbm(array):
    return pltpu.with_memory_space_constraint(array, pltpu.HBM)


def hbm():
    return pl.BlockSpec(memory_space=pltpu.HBM)


def start_loads(sources, targets, sems):
    copies = []
    for source, target in zip(sources, targets):
        pieces = 4 if source.shape[0] >= 512 else 1
        size = source.shape[0] // pieces
        for piece in range(pieces):
            cut = pl.ds(piece * size, size)
            copies.append(
                pltpu.make_async_copy(source.at[cut], target.at[cut], sems.at[len(copies)])
            )
    for copy in copies:
        copy.start()
    return copies


def load_kernel(place, hidden, w_query, w_key, w_value, own, query, key, value, sems, own_sem):
    rows = pl.ds(pl.multiple_of(place[0] * PIECE, PIECE), PIECE)
    copy = pltpu.make_async_copy(hidden.at[rows], own, own_sem)
    copy.start()
    copies = start_loads((w_key, w_value, w_query), (key, value, query), sems)
    copy.wait()
    for copy in copies:
        copy.wait()


def qkv_kernel(place, own, other, w_query, w_key, w_value, slots, normed):
    core = place[0]
    normed[:PIECE, :] = layer_norm(own[...].astype(f32)).astype(bf16)
    rows = pl.ds(pl.multiple_of(core * PIECE, PIECE), PIECE)
    normed[PIECE:, :] = layer_norm(other[rows, :].astype(f32)).astype(bf16)
    for column, weight in enumerate((w_query, w_key, w_value)):
        made = jnp.dot(normed[...], weight[...], preferred_element_type=f32)
        made = (made * POWER if column == 0 else made).astype(bf16)
        for part in range(2):
            sequence = core if part == 0 else 1 - core
            for head in range(HEADS):
                slots[sequence * HEADS + head, :, column * HEAD : (column + 1) * HEAD] = made[
                    part * PIECE : (part + 1) * PIECE, head * HEAD : (head + 1) * HEAD
                ]


def both_kernel(place, own, other, flow, other_flow, token, both):
    del token
    core = place[0]
    rows = pl.ds(pl.multiple_of(core * PIECE, PIECE), PIECE)
    both[:PIECE, :] = own[...]
    both[PIECE:TOKENS, :] = other[rows, :]
    both[TOKENS:, :] = jnp.zeros((CHANNELS, WIDTH), bf16)
    flows = []
    for source in (flow, other_flow):
        flows.append(jnp.where(core == 0, source[:, :PIECE].astype(f32), source[:, PIECE:].astype(f32)))
    both[TOKENS:, :TOKENS] = jnp.concatenate(flows, axis=1).astype(bf16)


def pack_kernel(slots, chunk, queries):
    for part in range(2):
        first = part * (PLANES // 2)
        base = part * ROWS
        values = []
        for plane in range(PLANES // 2):
            start = base + plane * PIECE
            chunk[start : start + PIECE, :] = slots[first + plane, :, HEAD : 2 * HEAD]
            values.append(slots[first + plane, :, 2 * HEAD :])
        values = jnp.concatenate(values, axis=0)
        for block in range(BLOCKS):
            square = values[block * HEAD : (block + 1) * HEAD, :].astype(f32)
            start = base + HALF + block * HEAD
            chunk[start : start + HEAD, :] = square.T.astype(bf16)
    queries[...] = slots[:, :, :HEAD]


def attend_kernel(chunks, first, last, after, *refs):
    refs = list(refs)
    place = refs.pop(0)
    if first:
        own, other = refs.pop(0), refs.pop(0)
    else:
        queries = refs.pop(0)
    segments = []
    for halves, source in chunks:
        chunk = refs.pop(0)
        for index, part in enumerate(halves):
            segments.append((chunk, index * ROWS, part, source))
    if not first:
        top_in, numer_in = refs.pop(0), refs.pop(0)
    refs = refs[after:]
    if first:
        queries = refs.pop(0)
        for tile in range(TILES):
            planes = (2 * tile, 2 * tile + 1)
            rows = [own[plane] for plane in planes] + [other[plane] for plane in planes]
            turned = jnp.concatenate(rows, axis=0).astype(f32).T
            queries[:, tile * TILE : (tile + 1) * TILE] = turned.astype(bf16)
    core = place[0]
    column = lax.broadcasted_iota(jnp.int32, (1, TILE), 1)
    column_half = jnp.where(column < TOKENS, core, 1 - core)
    column_plane = (column % TOKENS) // PIECE
    column_place = column_plane * (Z * TOKENS) + column_half * PIECE + column % PIECE
    key = lax.broadcasted_iota(jnp.int32, (HALF, 1), 0)
    key_place = (key // PIECE) * (Z * TOKENS) + key % PIECE + core * PIECE
    ones = jnp.ones((TALL - HEAD, HALF), bf16)
    values = []
    for chunk, base, _, _ in segments:
        starts = [base + HALF + index * HEAD for index in range(BLOCKS)]
        blocks = [chunk[start : start + HEAD, :] for start in starts]
        values.append(jnp.concatenate([jnp.concatenate(blocks, axis=1), ones], axis=0))

    def score(tile):
        columns = slice(tile * TILE, (tile + 1) * TILE)
        found = []
        for (chunk, base, part, source), value in zip(segments, values):
            groups = min(2, tile + 1 - 2 * part)
            if groups <= 0:
                continue
            count = groups * TOKENS
            product = jnp.dot(
                chunk[base : base + count, :], queries[:, columns], preferred_element_type=f32
            )
            if 2 * part + groups - 1 == tile:
                shift = place[1 + source] * TOKENS
                offset = 2 * (tile - 2 * part) * (Z * TOKENS)
                allowed = key_place[:count] + shift <= column_place + offset
                product = jnp.where(allowed, product, masked_score)
            found.append((value[:, :count], product))
        return found

    def finish(tile, found):
        columns = slice(tile * TILE, (tile + 1) * TILE)
        top = jnp.full((1, TILE), lowest, f32) if first else top_in[:1, columns]
        new_top = top
        for _, product in found:
            new_top = jnp.maximum(new_top, jnp.max(product, axis=0, keepdims=True))
        if first:
            sums = jnp.zeros((TALL, TILE), f32)
        else:
            sums = numer_in[:, columns] * jnp.exp2(top - new_top)
        for value, product in found:
            weights = jnp.exp2(product - new_top).astype(bf16)
            sums = sums + jnp.dot(value, weights, preferred_element_type=f32)
        if not last:
            top_out, numer_out = refs
            top_out[:, columns] = jnp.broadcast_to(new_top, (8, TILE))
            numer_out[:, columns] = sums
            return
        total = sums[HEAD : HEAD + 1, :]
        some = total > 0
        total = jnp.where(some, total, 1.0)
        mixed = (sums[:HEAD, :] / total).T
        level = jnp.where(some, new_top + jnp.log2(total), lowest)
        level = jnp.broadcast_to(level, (HEAD, TILE)).T
        high = level.astype(bf16)
        rest = level - high.astype(f32)
        middle = rest.astype(bf16)
        low = (rest - middle.astype(f32)).astype(bf16)
        lane = lax.broadcasted_iota(jnp.int32, (TILE, HEAD), 1)
        level = jnp.where(lane == 0, high, jnp.where(lane == 1, middle, low))
        for side in range(2):
            for plane in range(2):
                start = side * TOKENS + plane * PIECE
                refs[side][2 * tile + plane, :, :HEAD] = mixed[start : start + PIECE].astype(bf16)
                refs[side][2 * tile + plane, :, HEAD:] = level[start : start + PIECE]

    ahead = [score(0), score(1)]
    for tile in range(TILES):
        if tile + 2 < TILES:
            ahead.append(score(tile + 2))
        finish(tile, ahead.pop(0))


def attend(place, queries, segments, chunks, state, last, after=()):
    first = state is None
    count = sum(len(halves) for halves, _ in chunks)
    stats = [jax.ShapeDtypeStruct((8, 2 * ROWS), f32), jax.ShapeDtypeStruct((TALL, 2 * ROWS), f32)]
    if last:
        shapes = [jax.ShapeDtypeStruct((PLANES, PIECE, 2 * HEAD), bf16)] * 2
    elif first:
        shapes = [jax.ShapeDtypeStruct((HEAD, 2 * ROWS), bf16), *stats]
    else:
        shapes = stats
    operands = [place, *queries, *segments, *(state or ()), *after]
    return pl.pallas_call(
        functools.partial(attend_kernel, chunks, first, last, len(after)),
        out_shape=shapes,
        in_specs=[smem()] + [vmem()] * (len(operands) - 1),
        out_specs=[vmem()] * len(shapes),
        compiler_params=params(16),
        cost_estimate=pl.CostEstimate(
            flops=(FIRST_COST if first else COST) * ROWS * HALF * HEAD * count,
            bytes_accessed=3_000_000,
            transcendentals=ROWS * HALF * count,
        ),
    )(*operands)


def merge_kernel(mine, theirs, out):
    row = lax.broadcasted_iota(jnp.int32, (HEAD, HEAD), 0)
    spread = (row < 3).astype(f32).astype(bf16)

    def level(block):
        stats = block[:, :, HEAD:].reshape(ROWS, HEAD)
        return jnp.dot(stats, spread, preferred_element_type=f32)

    first, second = level(mine), level(theirs)
    top = jnp.maximum(first, second)
    first, second = jnp.exp2(first - top), jnp.exp2(second - top)
    both = first * mine[:, :, :HEAD].reshape(ROWS, HEAD).astype(f32)
    both = both + second * theirs[:, :, :HEAD].reshape(ROWS, HEAD).astype(f32)
    both = (both / (first + second)).astype(bf16).reshape(PLANES, PIECE, HEAD)
    for plane in range(PLANES):
        out[PLANES - 1 - plane] = both[plane]


FF_PARTS = 2
FF_PART = FF // FF_PARTS


def dense_kernel(
    place,
    attended,
    both,
    w_output,
    w_up,
    w_down,
    w_shift,
    w_scale,
    sent_own,
    sent_other,
):
    core = place[0]
    residual = both[:TOKENS, :].astype(f32)
    sides = []
    for sequence in (core, 1 - core):
        heads = [attended[sequence * HEADS + head] for head in range(HEADS)]
        sides.append(jnp.concatenate(heads, axis=1))
    mixed = jnp.concatenate(sides, axis=0)
    first = residual + jnp.dot(mixed, w_output[...], preferred_element_type=f32)
    inner = layer_norm(first).astype(bf16)
    second = first
    for part in range(FF_PARTS):
        cut = slice(part * FF_PART, (part + 1) * FF_PART)
        expanded = jnp.dot(inner, w_up[:, cut], preferred_element_type=f32)
        expanded = jax.nn.gelu(expanded).astype(bf16)
        second = second + jnp.dot(expanded, w_down[cut, :], preferred_element_type=f32)
    features = layer_norm(second).astype(bf16)
    shift, log_scale = (
        lax.dot_general(
            weight[...], features, (((1,), (1,)), ((), ())), preferred_element_type=f32
        )
        for weight in (w_shift, w_scale)
    )
    determinant = -jnp.sum(log_scale, axis=0, keepdims=True)
    high = determinant.astype(bf16)
    low = (determinant - high.astype(f32)).astype(bf16)
    row = lax.broadcasted_iota(jnp.int32, (SENT - CHANNELS, TOKENS), 0)
    tail = jnp.where(row == 0, high.astype(f32), jnp.where(row == 1, low.astype(f32), 0.0))
    flow = both[TOKENS:, :TOKENS].astype(f32)
    moved = (flow - shift) * jnp.exp(-log_scale)
    sent = jnp.concatenate([moved, tail], axis=0).astype(bf16)
    sent_own[...] = sent[:, :PIECE]
    sent_other[...] = sent[:, PIECE:]


def join_kernel(place, mine, theirs, out):
    core = place[0]
    row = lax.broadcasted_iota(jnp.int32, (PIECE, TOKENS), 0)
    column = lax.broadcasted_iota(jnp.int32, (PIECE, TOKENS), 1)
    total = None
    for source, half in ((mine, core), (theirs, 1 - core)):
        chosen = (column == TOKENS - 1 - half * PIECE - row).astype(f32).astype(bf16)
        term = jnp.dot(source[...], chosen, preferred_element_type=f32)
        total = term if total is None else total + term
    out[...] = total.astype(bf16)


def final_kernel(block, latent, log_det):
    latent[...] = block[:CHANNELS, :].astype(f32)
    det = block[CHANNELS:, :].astype(f32)
    log_det[...] = det[:1] + det[1:2]


def shift_by(count, step):
    return [(index, (index + step) % count) for index in range(count)]


def on_device(
    hidden, flow_input, w_query, w_key, w_value, w_output, w_up, w_down, w_shift, w_scale
):
    core = lax.axis_index("core")
    z = lax.axis_index("z")
    up_steps = [(z - step) % Z - z for step in range(5)]
    down_steps = [(z + step) % Z - z for step in range(4)]
    place = jnp.stack([core, *up_steps, *down_steps]).astype(jnp.int32)
    other_core = shift_by(2, 1)
    other = lax.ppermute(hidden, "core", other_core)
    other_flow = lax.ppermute(flow_input, "core", other_core)

    square = pltpu.VMEM((WIDTH, INNER), bf16)
    own, *weights = pl.pallas_call(
        load_kernel,
        out_shape=[pltpu.VMEM((PIECE, WIDTH), bf16), square, square, square],
        in_specs=[smem()] + [hbm()] * 4,
        out_specs=[vmem()] * 4,
        scratch_shapes=[pltpu.SemaphoreType.DMA((12,)), pltpu.SemaphoreType.DMA],
        compiler_params=params(8),
        cost_estimate=pl.CostEstimate(flops=0, bytes_accessed=6_600_000, transcendentals=0),
    )(place, *(in_hbm(array) for array in (hidden, w_query, w_key, w_value)))
    slots = pl.pallas_call(
        qkv_kernel,
        out_shape=jax.ShapeDtypeStruct((PLANES, PIECE, 3 * HEAD), bf16),
        in_specs=[smem()] + [vmem()] * 5,
        out_specs=vmem(),
        scratch_shapes=[pltpu.VMEM((TOKENS, WIDTH), bf16)],
        compiler_params=params(8),
    )(place, own, other, *weights)
    slots = lax.all_to_all(slots, ("xl", "y"), 0, 0, tiled=True)
    chunk, queries = pl.pallas_call(
        pack_kernel,
        out_shape=[
            jax.ShapeDtypeStruct((2 * ROWS, HEAD), bf16),
            jax.ShapeDtypeStruct((PLANES, PIECE, HEAD), bf16),
        ],
        in_specs=[vmem()],
        out_specs=[vmem()] * 2,
        compiler_params=params(8),
    )(slots)
    other_queries = lax.ppermute(queries, "core", other_core)

    whole = (0, 1)
    up = down = chunk
    queries, *state = attend(place, (queries, other_queries), [chunk], [(whole, 0)], None, False)
    both = pl.pallas_call(
        both_kernel,
        out_shape=jax.ShapeDtypeStruct((TOKENS + CHANNELS, WIDTH), bf16),
        in_specs=[smem()] + [vmem()] * 5,
        out_specs=vmem(),
        compiler_params=params(8),
    )(place, own, other, flow_input, other_flow, state[0])
    opposite = [(plane, PLANES - 1 - plane) for plane in range(PLANES)]
    both = lax.ppermute(both, ("xl", "y"), opposite)
    early = {AFTER: (both,)}
    for step in range(1, 4):
        up = lax.ppermute(up, "z", shift_by(Z, 1))
        down = lax.ppermute(down, "z", shift_by(Z, -1))
        state = attend(
            place,
            (queries,),
            [up, down],
            [(whole, step), (whole, 5 + step)],
            state,
            False,
            early.get(step, ()),
        )
    far = [
        lax.ppermute(up[:ROWS], "z", shift_by(Z, 1)),
        lax.ppermute(down[ROWS:], "z", shift_by(Z, -1)),
    ]
    mine, others = attend(place, (queries,), far, [((0,), 4), ((1,), 4)], state, True)
    theirs = lax.ppermute(others, "core", other_core)
    attended = pl.pallas_call(
        merge_kernel,
        out_shape=jax.ShapeDtypeStruct((PLANES, PIECE, HEAD), bf16),
        in_specs=[vmem()] * 2,
        out_specs=vmem(),
        compiler_params=params(8),
    )(mine, theirs)
    attended = lax.all_to_all(attended, ("xl", "y"), 0, 0, tiled=True)

    sent = jax.ShapeDtypeStruct((SENT, PIECE), bf16)
    sent_own, sent_other = pl.pallas_call(
        dense_kernel,
        out_shape=[sent, sent],
        in_specs=[smem()] + [vmem()] * 7,
        out_specs=[vmem()] * 2,
        compiler_params=params(16),
    )(
        place,
        attended,
        both,
        w_output,
        w_up,
        w_down,
        w_shift,
        w_scale,
    )
    received = lax.ppermute(sent_other, "core", other_core)
    block = pl.pallas_call(
        join_kernel,
        out_shape=jax.ShapeDtypeStruct((SENT, TOKENS), bf16),
        in_specs=[smem()] + [vmem()] * 2,
        out_specs=vmem(),
        compiler_params=params(8),
    )(place, sent_own, received)
    block = lax.ppermute(block, "z", [(index, Z - 1 - index) for index in range(Z)])
    latent, log_det = pl.pallas_call(
        final_kernel,
        out_shape=[
            jax.ShapeDtypeStruct((CHANNELS, TOKENS), f32),
            jax.ShapeDtypeStruct((1, TOKENS), f32),
        ],
        in_specs=[vmem()],
        out_specs=[vmem()] * 2,
        compiler_params=params(4),
    )(block)
    return (latent, log_det.reshape(TOKENS))


def solution(mesh):
    parts = Mesh(mesh.devices.reshape(2, 2, XL, Y, Z), ("xh", "core", "xl", "y", "z"))
    everywhere = ("xh", "core", "xl", "y", "z")
    in_specs = (P(everywhere, None), P(None, everywhere)) + (P(),) * 8
    out_specs = (P(None, everywhere), P(everywhere))
    return jax.shard_map(
        on_device, mesh=parts, in_specs=in_specs, out_specs=out_specs, check_vma=False
    )
```

```python
import functools

import jax
import jax.numpy as jnp
from jax import lax
from jax.experimental import pallas as pl
from jax.experimental.pallas import tpu as pltpu
from jax.sharding import Mesh, PartitionSpec as P

HEADS = 4
HEAD = 128
WIDTH = 1024
INNER = HEADS * HEAD
FF = 2048
CHANNELS = 64
epsilon = 1e-05
masked_score = -2e30
lowest = -1e30
POWER = HEAD**-0.5 * 1.4426950408889634
bf16 = jnp.bfloat16
f32 = jnp.float32

XL, Y, Z = 2, 4, 8
PLANES = XL * Y
TOKENS = 192
PIECE = TOKENS // 2
ROWS = PLANES * PIECE
TILE = 2 * TOKENS
TILES = 2 * ROWS // TILE
HALF = ROWS // 2
BLOCKS = HALF // HEAD
FIRST_COST, COST = 4, 32
AFTER = 2
TALL = HEAD + 16
SENT = CHANNELS + 16


def layer_norm(values):
    mean = jnp.mean(values, axis=-1, keepdims=True)
    centred = values - mean
    spread = jnp.mean(centred * centred, axis=-1, keepdims=True)
    return centred * lax.rsqrt(spread + epsilon)


def vmem():
    return pl.BlockSpec(memory_space=pltpu.VMEM)


def smem():
    return pl.BlockSpec(memory_space=pltpu.SMEM)


def params(mebibytes):
    return pltpu.CompilerParams(vmem_limit_bytes=mebibytes << 20)


def in_hbm(array):
    return pltpu.with_memory_space_constraint(array, pltpu.HBM)


def hbm():
    return pl.BlockSpec(memory_space=pltpu.HBM)


def start_loads(sources, targets, sems):
    copies = []
    for source, target in zip(sources, targets):
        pieces = 4 if source.shape[0] >= 512 else 1
        size = source.shape[0] // pieces
        for piece in range(pieces):
            cut = pl.ds(piece * size, size)
            copies.append(
                pltpu.make_async_copy(source.at[cut], target.at[cut], sems.at[len(copies)])
            )
    for copy in copies:
        copy.start()
    return copies


def load_kernel(
    place, hidden, w_query, w_key, w_value, own, own_normed, query, key, value, sems, own_sem
):
    rows = pl.ds(pl.multiple_of(place[0] * PIECE, PIECE), PIECE)
    copy = pltpu.make_async_copy(hidden.at[rows], own, own_sem)
    copy.start()
    copies = start_loads((w_key, w_value, w_query), (key, value, query), sems)
    copy.wait()
    own_normed[...] = layer_norm(own[...].astype(f32)).astype(bf16)
    for copy in copies:
        copy.wait()


def qkv_kernel(place, own_normed, other, w_query, w_key, w_value, slots, normed):
    core = place[0]
    normed[:PIECE, :] = own_normed[...]
    rows = pl.ds(pl.multiple_of(core * PIECE, PIECE), PIECE)
    normed[PIECE:, :] = layer_norm(other[rows, :].astype(f32)).astype(bf16)
    for column, weight in enumerate((w_query, w_key, w_value)):
        made = jnp.dot(normed[...], weight[...], preferred_element_type=f32)
        made = (made * POWER if column == 0 else made).astype(bf16)
        for part in range(2):
            sequence = core if part == 0 else 1 - core
            for head in range(HEADS):
                slots[sequence * HEADS + head, :, column * HEAD : (column + 1) * HEAD] = made[
                    part * PIECE : (part + 1) * PIECE, head * HEAD : (head + 1) * HEAD
                ]


def both_kernel(place, own, other, flow, other_flow, token, both):
    del token
    core = place[0]
    rows = pl.ds(pl.multiple_of(core * PIECE, PIECE), PIECE)
    both[:PIECE, :] = own[...]
    both[PIECE:TOKENS, :] = other[rows, :]
    both[TOKENS:, :] = jnp.zeros((CHANNELS, WIDTH), bf16)
    flows = []
    for source in (flow, other_flow):
        flows.append(jnp.where(core == 0, source[:, :PIECE].astype(f32), source[:, PIECE:].astype(f32)))
    both[TOKENS:, :TOKENS] = jnp.concatenate(flows, axis=1).astype(bf16)


def pack_kernel(slots, chunk, queries):
    for part in range(2):
        first = part * (PLANES // 2)
        base = part * ROWS
        values = []
        for plane in range(PLANES // 2):
            start = base + plane * PIECE
            chunk[start : start + PIECE, :] = slots[first + plane, :, HEAD : 2 * HEAD]
            values.append(slots[first + plane, :, 2 * HEAD :])
        values = jnp.concatenate(values, axis=0)
        for block in range(BLOCKS):
            square = values[block * HEAD : (block + 1) * HEAD, :].astype(f32)
            start = base + HALF + block * HEAD
            chunk[start : start + HEAD, :] = square.T.astype(bf16)
    queries[...] = slots[:, :, :HEAD]


def attend_kernel(chunks, first, last, after, *refs):
    refs = list(refs)
    place = refs.pop(0)
    if first:
        own, other = refs.pop(0), refs.pop(0)
    else:
        queries = refs.pop(0)
    segments = []
    for halves, source in chunks:
        chunk = refs.pop(0)
        for index, part in enumerate(halves):
            segments.append((chunk, index * ROWS, part, source))
    if not first:
        top_in, numer_in = refs.pop(0), refs.pop(0)
    refs = refs[after:]
    if first:
        queries = refs.pop(0)
        for tile in range(TILES):
            planes = (2 * tile, 2 * tile + 1)
            rows = [own[plane] for plane in planes] + [other[plane] for plane in planes]
            turned = jnp.concatenate(rows, axis=0).astype(f32).T
            queries[:, tile * TILE : (tile + 1) * TILE] = turned.astype(bf16)
    core = place[0]
    column = lax.broadcasted_iota(jnp.int32, (1, TILE), 1)
    column_half = jnp.where(column < TOKENS, core, 1 - core)
    column_plane = (column % TOKENS) // PIECE
    column_place = column_plane * (Z * TOKENS) + column_half * PIECE + column % PIECE
    key = lax.broadcasted_iota(jnp.int32, (HALF, 1), 0)
    key_place = (key // PIECE) * (Z * TOKENS) + key % PIECE + core * PIECE
    ones = jnp.ones((TALL - HEAD, HALF), bf16)
    values = []
    for chunk, base, _, _ in segments:
        starts = [base + HALF + index * HEAD for index in range(BLOCKS)]
        blocks = [chunk[start : start + HEAD, :] for start in starts]
        values.append(jnp.concatenate([jnp.concatenate(blocks, axis=1), ones], axis=0))

    def score(tile):
        columns = slice(tile * TILE, (tile + 1) * TILE)
        found = []
        for (chunk, base, part, source), value in zip(segments, values):
            groups = min(2, tile + 1 - 2 * part)
            if groups <= 0:
                continue
            count = groups * TOKENS
            product = jnp.dot(
                chunk[base : base + count, :], queries[:, columns], preferred_element_type=f32
            )
            if 2 * part + groups - 1 == tile:
                shift = place[1 + source] * TOKENS
                offset = 2 * (tile - 2 * part) * (Z * TOKENS)
                allowed = key_place[:count] + shift <= column_place + offset
                product = jnp.where(allowed, product, masked_score)
            found.append((value[:, :count], product))
        return found

    def finish(tile, found):
        columns = slice(tile * TILE, (tile + 1) * TILE)
        top = jnp.full((1, TILE), lowest, f32) if first else top_in[:1, columns]
        new_top = top
        for _, product in found:
            new_top = jnp.maximum(new_top, jnp.max(product, axis=0, keepdims=True))
        if first:
            sums = jnp.zeros((TALL, TILE), f32)
        else:
            sums = numer_in[:, columns] * jnp.exp2(top - new_top)
        for value, product in found:
            weights = jnp.exp2(product - new_top).astype(bf16)
            sums = sums + jnp.dot(value, weights, preferred_element_type=f32)
        if not last:
            top_out, numer_out = refs
            top_out[:, columns] = jnp.broadcast_to(new_top, (8, TILE))
            numer_out[:, columns] = sums
            return
        total = sums[HEAD : HEAD + 1, :]
        some = total > 0
        total = jnp.where(some, total, 1.0)
        mixed = (sums[:HEAD, :] / total).T
        level = jnp.where(some, new_top + jnp.log2(total), lowest)
        level = jnp.broadcast_to(level, (HEAD, TILE)).T
        high = level.astype(bf16)
        rest = level - high.astype(f32)
        middle = rest.astype(bf16)
        low = (rest - middle.astype(f32)).astype(bf16)
        lane = lax.broadcasted_iota(jnp.int32, (TILE, HEAD), 1)
        level = jnp.where(lane == 0, high, jnp.where(lane == 1, middle, low))
        for side in range(2):
            for plane in range(2):
                start = side * TOKENS + plane * PIECE
                refs[side][2 * tile + plane, :, :HEAD] = mixed[start : start + PIECE].astype(bf16)
                refs[side][2 * tile + plane, :, HEAD:] = level[start : start + PIECE]

    ahead = [score(0), score(1)]
    for tile in range(TILES):
        if tile + 2 < TILES:
            ahead.append(score(tile + 2))
        finish(tile, ahead.pop(0))


def attend(place, queries, segments, chunks, state, last, after=()):
    first = state is None
    count = sum(len(halves) for halves, _ in chunks)
    stats = [jax.ShapeDtypeStruct((8, 2 * ROWS), f32), jax.ShapeDtypeStruct((TALL, 2 * ROWS), f32)]
    if last:
        shapes = [jax.ShapeDtypeStruct((PLANES, PIECE, 2 * HEAD), bf16)] * 2
    elif first:
        shapes = [jax.ShapeDtypeStruct((HEAD, 2 * ROWS), bf16), *stats]
    else:
        shapes = stats
    operands = [place, *queries, *segments, *(state or ()), *after]
    return pl.pallas_call(
        functools.partial(attend_kernel, chunks, first, last, len(after)),
        out_shape=shapes,
        in_specs=[smem()] + [vmem()] * (len(operands) - 1),
        out_specs=[vmem()] * len(shapes),
        compiler_params=params(16),
        cost_estimate=pl.CostEstimate(
            flops=(FIRST_COST if first else COST) * ROWS * HALF * HEAD * count,
            bytes_accessed=3_000_000,
            transcendentals=ROWS * HALF * count,
        ),
    )(*operands)


def merge_kernel(mine, theirs, out):
    row = lax.broadcasted_iota(jnp.int32, (HEAD, HEAD), 0)
    spread = (row < 3).astype(f32).astype(bf16)

    def level(block):
        stats = block[:, :, HEAD:].reshape(ROWS, HEAD)
        return jnp.dot(stats, spread, preferred_element_type=f32)

    first, second = level(mine), level(theirs)
    top = jnp.maximum(first, second)
    first, second = jnp.exp2(first - top), jnp.exp2(second - top)
    both = first * mine[:, :, :HEAD].reshape(ROWS, HEAD).astype(f32)
    both = both + second * theirs[:, :, :HEAD].reshape(ROWS, HEAD).astype(f32)
    both = (both / (first + second)).astype(bf16).reshape(PLANES, PIECE, HEAD)
    for plane in range(PLANES):
        out[PLANES - 1 - plane] = both[plane]


FF_PARTS = 2
FF_PART = FF // FF_PARTS


def dense_kernel(
    place,
    attended,
    both,
    w_output,
    w_up,
    w_down,
    w_shift,
    w_scale,
    sent_own,
    sent_other,
):
    core = place[0]
    residual = both[:TOKENS, :].astype(f32)
    sides = []
    for sequence in (core, 1 - core):
        heads = [attended[sequence * HEADS + head] for head in range(HEADS)]
        sides.append(jnp.concatenate(heads, axis=1))
    mixed = jnp.concatenate(sides, axis=0)
    first = residual + jnp.dot(mixed, w_output[...], preferred_element_type=f32)
    inner = layer_norm(first).astype(bf16)
    second = first
    for part in range(FF_PARTS):
        cut = slice(part * FF_PART, (part + 1) * FF_PART)
        expanded = jnp.dot(inner, w_up[:, cut], preferred_element_type=f32)
        expanded = jax.nn.gelu(expanded).astype(bf16)
        second = second + jnp.dot(expanded, w_down[cut, :], preferred_element_type=f32)
    features = layer_norm(second).astype(bf16)
    shift, log_scale = (
        lax.dot_general(
            weight[...], features, (((1,), (1,)), ((), ())), preferred_element_type=f32
        )
        for weight in (w_shift, w_scale)
    )
    determinant = -jnp.sum(log_scale, axis=0, keepdims=True)
    high = determinant.astype(bf16)
    low = (determinant - high.astype(f32)).astype(bf16)
    row = lax.broadcasted_iota(jnp.int32, (SENT - CHANNELS, TOKENS), 0)
    tail = jnp.where(row == 0, high.astype(f32), jnp.where(row == 1, low.astype(f32), 0.0))
    flow = both[TOKENS:, :TOKENS].astype(f32)
    moved = (flow - shift) * jnp.exp(-log_scale)
    sent = jnp.concatenate([moved, tail], axis=0).astype(bf16)
    sent_own[...] = sent[:, :PIECE]
    sent_other[...] = sent[:, PIECE:]


def join_kernel(place, mine, theirs, out):
    core = place[0]
    row = lax.broadcasted_iota(jnp.int32, (PIECE, TOKENS), 0)
    column = lax.broadcasted_iota(jnp.int32, (PIECE, TOKENS), 1)
    total = None
    for source, half in ((mine, core), (theirs, 1 - core)):
        chosen = (column == TOKENS - 1 - half * PIECE - row).astype(f32).astype(bf16)
        term = jnp.dot(source[...], chosen, preferred_element_type=f32)
        total = term if total is None else total + term
    out[...] = total.astype(bf16)


def final_kernel(block, latent, log_det):
    latent[...] = block[:CHANNELS, :].astype(f32)
    det = block[CHANNELS:, :].astype(f32)
    log_det[...] = det[:1] + det[1:2]


def shift_by(count, step):
    return [(index, (index + step) % count) for index in range(count)]


def on_device(
    hidden, flow_input, w_query, w_key, w_value, w_output, w_up, w_down, w_shift, w_scale
):
    core = lax.axis_index("core")
    z = lax.axis_index("z")
    up_steps = [(z - step) % Z - z for step in range(5)]
    down_steps = [(z + step) % Z - z for step in range(4)]
    place = jnp.stack([core, *up_steps, *down_steps]).astype(jnp.int32)
    other_core = shift_by(2, 1)
    other = lax.ppermute(hidden, "core", other_core)
    other_flow = lax.ppermute(flow_input, "core", other_core)

    square = pltpu.VMEM((WIDTH, INNER), bf16)
    own, own_normed, *weights = pl.pallas_call(
        load_kernel,
        out_shape=[pltpu.VMEM((PIECE, WIDTH), bf16)] * 2 + [square] * 3,
        in_specs=[smem()] + [hbm()] * 4,
        out_specs=[vmem()] * 5,
        scratch_shapes=[pltpu.SemaphoreType.DMA((12,)), pltpu.SemaphoreType.DMA],
        compiler_params=params(8),
        cost_estimate=pl.CostEstimate(flops=0, bytes_accessed=6_600_000, transcendentals=0),
    )(place, *(in_hbm(array) for array in (hidden, w_query, w_key, w_value)))
    slots = pl.pallas_call(
        qkv_kernel,
        out_shape=jax.ShapeDtypeStruct((PLANES, PIECE, 3 * HEAD), bf16),
        in_specs=[smem()] + [vmem()] * 5,
        out_specs=vmem(),
        scratch_shapes=[pltpu.VMEM((TOKENS, WIDTH), bf16)],
        compiler_params=params(8),
    )(place, own_normed, other, *weights)
    slots = lax.all_to_all(slots, ("xl", "y"), 0, 0, tiled=True)
    chunk, queries = pl.pallas_call(
        pack_kernel,
        out_shape=[
            jax.ShapeDtypeStruct((2 * ROWS, HEAD), bf16),
            jax.ShapeDtypeStruct((PLANES, PIECE, HEAD), bf16),
        ],
        in_specs=[vmem()],
        out_specs=[vmem()] * 2,
        compiler_params=params(8),
    )(slots)
    other_queries = lax.ppermute(queries, "core", other_core)

    whole = (0, 1)
    up = down = chunk
    queries, *state = attend(place, (queries, other_queries), [chunk], [(whole, 0)], None, False)
    both = pl.pallas_call(
        both_kernel,
        out_shape=jax.ShapeDtypeStruct((TOKENS + CHANNELS, WIDTH), bf16),
        in_specs=[smem()] + [vmem()] * 5,
        out_specs=vmem(),
        compiler_params=params(8),
    )(place, own, other, flow_input, other_flow, state[0])
    opposite = [(plane, PLANES - 1 - plane) for plane in range(PLANES)]
    both = lax.ppermute(both, ("xl", "y"), opposite)
    early = {AFTER: (both,)}
    for step in range(1, 4):
        up = lax.ppermute(up, "z", shift_by(Z, 1))
        down = lax.ppermute(down, "z", shift_by(Z, -1))
        state = attend(
            place,
            (queries,),
            [up, down],
            [(whole, step), (whole, 5 + step)],
            state,
            False,
            early.get(step, ()),
        )
    far = [
        lax.ppermute(up[:ROWS], "z", shift_by(Z, 1)),
        lax.ppermute(down[ROWS:], "z", shift_by(Z, -1)),
    ]
    mine, others = attend(place, (queries,), far, [((0,), 4), ((1,), 4)], state, True)
    theirs = lax.ppermute(others, "core", other_core)
    attended = pl.pallas_call(
        merge_kernel,
        out_shape=jax.ShapeDtypeStruct((PLANES, PIECE, HEAD), bf16),
        in_specs=[vmem()] * 2,
        out_specs=vmem(),
        compiler_params=params(8),
    )(mine, theirs)
    attended = lax.all_to_all(attended, ("xl", "y"), 0, 0, tiled=True)

    sent = jax.ShapeDtypeStruct((SENT, PIECE), bf16)
    sent_own, sent_other = pl.pallas_call(
        dense_kernel,
        out_shape=[sent, sent],
        in_specs=[smem()] + [vmem()] * 7,
        out_specs=[vmem()] * 2,
        compiler_params=params(16),
    )(
        place,
        attended,
        both,
        w_output,
        w_up,
        w_down,
        w_shift,
        w_scale,
    )
    received = lax.ppermute(sent_other, "core", other_core)
    block = pl.pallas_call(
        join_kernel,
        out_shape=jax.ShapeDtypeStruct((SENT, TOKENS), bf16),
        in_specs=[smem()] + [vmem()] * 2,
        out_specs=vmem(),
        compiler_params=params(8),
    )(place, sent_own, received)
    block = lax.ppermute(block, "z", [(index, Z - 1 - index) for index in range(Z)])
    latent, log_det = pl.pallas_call(
        final_kernel,
        out_shape=[
            jax.ShapeDtypeStruct((CHANNELS, TOKENS), f32),
            jax.ShapeDtypeStruct((1, TOKENS), f32),
        ],
        in_specs=[vmem()],
        out_specs=[vmem()] * 2,
        compiler_params=params(4),
    )(block)
    return (latent, log_det.reshape(TOKENS))


def solution(mesh):
    parts = Mesh(mesh.devices.reshape(2, 2, XL, Y, Z), ("xh", "core", "xl", "y", "z"))
    everywhere = ("xh", "core", "xl", "y", "z")
    in_specs = (P(everywhere, None), P(None, everywhere)) + (P(),) * 8
    out_specs = (P(None, everywhere), P(everywhere))
    return jax.shard_map(
        on_device, mesh=parts, in_specs=in_specs, out_specs=out_specs, check_vma=False
    )
```
